256 devices in a mesh: tm: 64 (over x, z, core), items: 4 (over y).
Axes of the slice: x: 4, y: 4, z: 8, core: 2. Of those that a mesh axis runs over, the one named last changes fastest.
Arguments:
- production: float32 [3072, 16384], P('tm', 'items'), may hold values from 0 to 2
- setup: float32 [3072, 16384], P('tm', 'items'), may hold values from 0 to 1
- shortage: float32 [3072, 16384], P('tm', 'items'), may hold values from 0 to 1
- dual_demand: float32 [3072, 16384], P('tm', 'items'), may hold values from 0.05 to 2
- dual_link: float32 [3072, 16384], P('tm', 'items'), may hold values from 0.05 to 1
- dual_resource: float32 [3072, 128], P('tm'), may hold values from 0.05 to 1
- cost_production: float32 [3072, 16384], P('tm', 'items'), may hold values from 0.1 to 2
- cost_setup: float32 [16384], P('items'), may hold values from 0.5 to 4
- penalty: float32 [16384], P('items'), may hold values from 1 to 8
- demand: float32 [3072, 16384], P('tm', 'items'), may hold values from 0.2 to 1.5
- capacity: float32 [3072, 128], P('tm'), may hold values from 12.8 to 64
- coef_production: float32 [256, 128], replicated, may hold values from 0.0015625 to 0.015625
- coef_setup: float32 [256, 128], replicated, may hold values from 0.0015625 to 0.015625
- horizon_start: int32 [16384], P('items'), may hold values from 0 to 3071, as said below
- horizon_end: int32 [16384], P('items'), may hold values from 0 to 3071, as said below
- fixing: int32 [3072, 16384], P('tm', 'items'), may hold values from 0 to 2
- block_id: int32 [16384], P('items'), may hold values from 0 to 255
Outputs:
- production_next: float32 [3072, 16384], P('tm', 'items')
- setup_next: float32 [3072, 16384], P('tm', 'items')
- shortage_next: float32 [3072, 16384], P('tm', 'items')
- dual_demand_next: float32 [3072, 16384], P('tm', 'items')
- dual_link_next: float32 [3072, 16384], P('tm', 'items')
- dual_resource_next: float32 [3072, 128], P('tm')
The draws below stay inside these ranges and needn't reach their ends.
Inputs may be any that keep to these rules, and one draw needn't show every extreme that they name: horizon_start[i] <= horizon_end[i] for every item; some item's horizon starts in the first period. `horizon_end`: some item's horizon ends in the last period.
All inputs are finite; a program needn't handle non-finite values.
Results may differ from the reference program's by a relative error of at most 0.00007.
Values sent between devices are 32-bit elements; how exact they have to be, the bound alone decides.
A program may use at most 64 MiB of HBM per device.

```python
import math
import jax
import jax.numpy as jnp
from jax import lax

RES = 128
NBLK = 256
PERIODS = 3072
ITEMS = 16384


def window_pair(key):
    first_key, second_key = jax.random.split(key)
    left_end = jax.random.randint(first_key, (ITEMS,), 0, PERIODS)
    right_end = jax.random.randint(second_key, (ITEMS,), 0, PERIODS)
    lower = jnp.minimum(left_end, right_end).at[0].set(0)
    upper = jnp.maximum(left_end, right_end).at[0].set(PERIODS - 1)
    return (lower.astype(jnp.int32), upper.astype(jnp.int32))


def draw_horizon_start(key, part):
    return window_pair(key)[0]


def draw_horizon_end(key, part):
    return window_pair(key)[1]


def place_ends(entries, key, low, largest):
    extent = entries.shape
    spot = [jax.random.randint(jax.random.fold_in(key, axis), (), 0, extent[axis]) for axis in range(len(extent))]
    entries = entries.at[tuple(spot)].set(low)
    longest = extent.index(max(extent))
    spot[longest] = (spot[longest] + 1) % extent[longest]
    return entries.at[tuple(spot)].set(largest)


def block_scale(key, dims, shards, least, high):
    def one(axis_at, parts):
        heights = jax.random.uniform(jax.random.fold_in(jax.random.fold_in(key, 6), axis_at), (parts,), jnp.float32, least / len(shards), high / len(shards))
        return jnp.repeat(jnp.exp(heights), dims[axis_at] // parts).reshape((-1,) + (1,) * (len(dims) - axis_at - 1))

    factor_of = one(*shards[0])
    for cut in shards[1:]:
        factor_of = factor_of * one(*cut)
    return factor_of


def setup_inputs(seed: int = 0) -> dict:
    splits = jax.random.split(jax.random.key(seed), 18)
    production = jnp.clip(2.0 * jax.random.uniform(splits[0], (PERIODS, ITEMS), jnp.float32) ** block_scale(splits[0], (PERIODS, ITEMS), ((0, 64), (1, 4)), -0.2, 0.2), 0.0, 2.0)
    setup = jnp.clip(1.0 * jax.random.uniform(splits[1], (PERIODS, ITEMS), jnp.float32) ** block_scale(splits[1], (PERIODS, ITEMS), ((0, 64), (1, 4)), -0.2, 0.2), 0.0, 1.0)
    shortage = jnp.clip(1.0 * jax.random.uniform(splits[2], (PERIODS, ITEMS), jnp.float32) ** block_scale(splits[2], (PERIODS, ITEMS), ((0, 64), (1, 4)), -0.2, 0.2), 0.0, 1.0)
    dual_demand = jnp.clip(jnp.exp(math.log(2.0) - 3.6888794 * jax.random.uniform(splits[3], (PERIODS, ITEMS), jnp.float32) ** block_scale(splits[3], (PERIODS, ITEMS), ((0, 64), (1, 4)), -0.2, 0.2)), 0.05, 2.0)
    dual_link = jnp.clip(jnp.exp(math.log(1.0) - 2.9957323 * jax.random.uniform(splits[4], (PERIODS, ITEMS), jnp.float32) ** block_scale(splits[4], (PERIODS, ITEMS), ((0, 64), (1, 4)), -0.2, 0.2)), 0.05, 1.0)
    dual_resource = jnp.clip(jnp.exp(math.log(1.0) - 2.9957323 * jax.random.uniform(splits[5], (PERIODS, RES), jnp.float32) ** block_scale(splits[5], (PERIODS, RES), ((0, 64),), -0.2, 0.2)), 0.05, 1.0)
    cost_production = jnp.clip(jnp.exp(math.log(2.0) - 2.9957323 * jax.random.uniform(splits[6], (PERIODS, ITEMS), jnp.float32) ** block_scale(splits[6], (PERIODS, ITEMS), ((0, 64), (1, 4)), -0.2, 0.2)), 0.1, 2.0)
    cost_setup = jnp.clip(jnp.exp(math.log(4.0) - 2.0794415 * jax.random.uniform(splits[7], (ITEMS,), jnp.float32) ** block_scale(splits[7], (ITEMS,), ((0, 4),), -0.2, 0.2)), 0.5, 4.0)
    penalty = jnp.clip(jnp.exp(math.log(8.0) - 2.0794415 * jax.random.uniform(splits[8], (ITEMS,), jnp.float32) ** block_scale(splits[8], (ITEMS,), ((0, 4),), -0.2, 0.2)), 1.0, 8.0)
    demand = jnp.clip(0.2 + 1.3 * jax.random.uniform(splits[9], (PERIODS, ITEMS), jnp.float32) ** block_scale(splits[9], (PERIODS, ITEMS), ((0, 64), (1, 4)), -0.2, 0.2), 0.2, 1.5)
    capacity = jnp.clip(12.8 + 51.2 * jax.random.uniform(splits[10], (PERIODS, RES), jnp.float32) ** block_scale(splits[10], (PERIODS, RES), ((0, 64),), -0.2, 0.2), 12.8, 64.0)
    coef_production = jnp.clip(jnp.exp(jax.random.uniform(splits[11], (NBLK, RES), jnp.float32, math.log(0.0015625), math.log(0.015625))), 0.0015625, 0.015625)
    coef_setup = jnp.clip(jnp.exp(jax.random.uniform(splits[12], (NBLK, RES), jnp.float32, math.log(0.0015625), math.log(0.015625))), 0.0015625, 0.015625)
    horizon_start = draw_horizon_start(jax.random.fold_in(splits[17], 71), 0)
    horizon_end = draw_horizon_end(jax.random.fold_in(splits[17], 71), 0)
    fixing = place_ends(jax.random.randint(splits[15], (PERIODS, ITEMS), 0, 3), jax.random.fold_in(splits[15], 1), 0, 2).astype(jnp.int32)
    block_id = place_ends(jax.random.randint(splits[16], (ITEMS,), 0, NBLK), jax.random.fold_in(splits[16], 1), 0, NBLK - 1).astype(jnp.int32)
    return {"production": production, "setup": setup, "shortage": shortage, "dual_demand": dual_demand, "dual_link": dual_link, "dual_resource": dual_resource, "cost_production": cost_production, "cost_setup": cost_setup, "penalty": penalty, "demand": demand, "capacity": capacity, "coef_production": coef_production, "coef_setup": coef_setup, "horizon_start": horizon_start, "horizon_end": horizon_end, "fixing": fixing, "block_id": block_id}


big_m = 4.0
setup_step = 0.5
short_step = 0.5
link_step = 0.25


def product(left, right):
    return jnp.dot(left, right, precision=lax.Precision.HIGHEST, preferred_element_type=jnp.float32)


def reference(production, setup, shortage, dual_demand, dual_link, dual_resource, cost_production, cost_setup, penalty, demand, capacity, coef_production, coef_setup, horizon_start, horizon_end, fixing, block_id):
    period = lax.broadcasted_iota(jnp.int32, (PERIODS, ITEMS), 0)
    active = ((period >= horizon_start[None, :]) & (period <= horizon_end[None, :])).astype(jnp.float32)
    onehot = (block_id[:, None] == lax.broadcasted_iota(jnp.int32, (ITEMS, NBLK), 1)).astype(jnp.float32)
    dual_active = dual_demand * active
    link_active = dual_link * active
    suffix = jnp.cumsum(dual_active[::-1], axis=0)[::-1]
    primal_step = 1.0 / (2.0 + jnp.maximum(horizon_end[None, :] - period, 0).astype(jnp.float32))
    dual_step = 1.0 / (2.0 + jnp.maximum(period - horizon_start[None, :], 0).astype(jnp.float32))
    pull_prod = product(product(dual_resource, coef_production.T), onehot.T)
    pull_setup = product(product(dual_resource, coef_setup.T), onehot.T)
    production_next = jnp.maximum(production - primal_step * (cost_production - suffix + link_active + pull_prod), 0.0) * active
    moved = jnp.clip(setup - setup_step * (cost_setup[None, :] - big_m * link_active + pull_setup), 0.0, 1.0)
    moved = jnp.where(fixing == 1, 0.0, jnp.where(fixing == 2, 1.0, moved))
    setup_next = moved * active
    shortage_next = jnp.maximum(shortage - short_step * (penalty[None, :] - dual_active), 0.0) * active
    prod_bar = (2.0 * production_next - production) * active
    setup_bar = (2.0 * setup_next - setup) * active
    short_bar = (2.0 * shortage_next - shortage) * active
    inventory = jnp.cumsum((prod_bar - demand) * active, axis=0)
    dual_demand_next = jnp.maximum(dual_active - dual_step * (inventory + short_bar), 0.0) * active
    dual_link_next = jnp.maximum(link_active + link_step * (prod_bar - big_m * setup_bar), 0.0) * active
    usage_all = product(product(prod_bar, onehot), coef_production) + product(product(setup_bar, onehot), coef_setup)
    dual_resource_next = jnp.maximum(dual_resource + (RES / ITEMS) * (usage_all - capacity), 0.0)
    return production_next, setup_next, shortage_next, dual_demand_next, dual_link_next, dual_resource_next
```

```python
import functools

import jax
import jax.numpy as jnp
from jax import lax
from jax.experimental import pallas as pl
from jax.experimental.pallas import tpu as pltpu
from jax.sharding import PartitionSpec as P

MESH = pl.DeviceIdType.MESH
F32 = jnp.float32
BF16 = jnp.bfloat16

big_m = 4.0
setup_step = 0.5
short_step = 0.5
link_step = 0.25

LANES = 128
GROUP = 8
CORES = 2
DEPTH = 8


def suffix_rows(groups, sub):
    tail = jnp.zeros((GROUP, LANES), F32)
    out = [None] * len(groups)
    for g in reversed(range(len(groups))):
        part = groups[g]
        for shift in (1, 2, 4):
            moved = pltpu.roll(part, GROUP - shift, 0)
            part = part + jnp.where(sub < GROUP - shift, moved, 0.0)
        out[g] = part + tail
        tail = jnp.broadcast_to(out[g][0:1, :], (GROUP, LANES))
    return out, tail


def prefix_rows(groups, sub):
    head = jnp.zeros((GROUP, LANES), F32)
    out = [None] * len(groups)
    for g in range(len(groups)):
        part = groups[g]
        for shift in (1, 2, 4):
            moved = pltpu.roll(part, shift, 0)
            part = part + jnp.where(sub >= shift, moved, 0.0)
        out[g] = part + head
        head = jnp.broadcast_to(out[g][GROUP - 1 :, :], (GROUP, LANES))
    return out


def halves(value, count):
    terms = []
    for k in range(count):
        term = value.astype(BF16)
        terms.append(term)
        if k + 1 < count:
            value = value - term.astype(F32)
    return terms


def exact(left, right, contract):
    return lax.dot_general(
        left, right, (contract, ((), ())), precision=lax.Precision.HIGHEST, preferred_element_type=F32
    )


def kernel(
    ranks,
    items_total,
    production_h,
    setup_h,
    shortage_h,
    dual_demand_h,
    dual_link_h,
    dual_resource_h,
    cost_production_h,
    cost_setup_h,
    penalty_h,
    demand_h,
    capacity_h,
    coef_production_h,
    coef_setup_h,
    start_h,
    end_h,
    fixing_h,
    block_h,
    production_o,
    setup_o,
    shortage_o,
    dual_demand_o,
    dual_link_o,
    dual_resource_o,
    production_v,
    setup_v,
    shortage_v,
    dual_demand_v,
    dual_link_v,
    cost_production_v,
    demand_v,
    fixing_v,
    dual_resource_v,
    capacity_v,
    coef_production_v,
    coef_setup_v,
    cost_setup_v,
    penalty_v,
    start_v,
    end_v,
    block_v,
    start_f,
    end_f,
    onehot_v,
    pull_production_v,
    pull_setup_v,
    local_v,
    primal_step_v,
    dual_step_v,
    setup_bar_v,
    prod_bar_v,
    link_v,
    flow_v,
    own_v,
    sibling_v,
    along_z_v,
    along_x_v,
    inside_v,
    carry_v,
    usage_v,
    in_sem,
    out_sem,
    core_send,
    core_recv,
    z_send,
    z_recv,
    x_send,
    x_recv,
    inside_send,
    inside_recv,
    y_send,
    y_recv,
):
    nx, nz, ny = ranks
    rows, items = production_v.shape
    groups = rows // GROUP
    chunks = items // LANES
    half = chunks // 2
    blocks = coef_production_v.shape[0]
    tm = lax.axis_index("tm")
    y = lax.axis_index("items")
    core = lax.rem(tm, CORES)
    z = lax.rem(tm // CORES, nz)
    x = tm // (CORES * nz)

    def place(px, pz, pc, py=None):
        return ((px * nz + pz) * CORES + pc, y if py is None else py)

    loads = [
        (start_h, start_v),
        (end_h, end_v),
        (dual_demand_h, dual_demand_v),
        (block_h, block_v),
        (dual_resource_h, dual_resource_v),
        (coef_production_h, coef_production_v),
        (coef_setup_h, coef_setup_v),
        (cost_setup_h, cost_setup_v),
        (penalty_h, penalty_v),
        (dual_link_h, dual_link_v),
        (setup_h, setup_v),
        (fixing_h, fixing_v),
        (shortage_h, shortage_v),
        (production_h, production_v),
        (cost_production_h, cost_production_v),
        (demand_h, demand_v),
        (capacity_h, capacity_v),
    ]
    load = [pltpu.make_async_copy(src, dst, in_sem.at[k]) for k, (src, dst) in enumerate(loads)]
    for copy in load:
        copy.start()

    barrier = pltpu.get_barrier_semaphore()
    greeted = 0
    for d in range(1, nz):
        pl.semaphore_signal(
            barrier, inc=1, device_id=place(x, lax.rem(z + d, nz), core), device_id_type=MESH
        )
        greeted += 1
    for d in range(1, nx):
        for c in range(CORES):
            pl.semaphore_signal(
                barrier, inc=1, device_id=place(lax.rem(x + d, nx), z, c), device_id_type=MESH
            )
            greeted += 1
    for d in range(1, ny):
        pl.semaphore_signal(
            barrier, inc=1, device_id=place(x, z, core, lax.rem(y + d, ny)), device_id_type=MESH
        )
        greeted += 1
    pl.semaphore_signal(barrier, inc=1, device_id=place(x, z, 1 - core), device_id_type=MESH)
    greeted += 1

    sub = lax.broadcasted_iota(jnp.int32, (GROUP, LANES), 0)
    first = (tm * rows).astype(F32)
    period = [sub.astype(F32) + (first + float(g * GROUP)) for g in range(groups)]

    def lanes(j):
        return pl.ds(pl.multiple_of(j * LANES, LANES), LANES)

    def piece(ref, g, j):
        return ref[g * GROUP : (g + 1) * GROUP, lanes(j)]

    def put(ref, g, j, value):
        ref[g * GROUP : (g + 1) * GROUP, lanes(j)] = value

    def row(ref, j):
        return jnp.broadcast_to(ref[pl.ds(j, 1), :], (GROUP, LANES))

    def window(j):
        begin, stop = row(start_f, j), row(end_f, j)
        return begin, stop, [(t >= begin) & (t <= stop) for t in period]

    load[0].wait()
    load[1].wait()
    start_f[...] = start_v[...].astype(F32)
    end_f[...] = end_v[...].astype(F32)

    load[2].wait()

    @pl.loop(0, chunks)
    def _(j):
        begin, stop, active = window(j)
        parts = [jnp.where(active[g], piece(dual_demand_v, g, j), 0.0) for g in range(groups)]
        tails, total = suffix_rows(parts, sub)
        for g in range(groups):
            put(local_v, g, j, tails[g])
        own_v[0, pl.ds(j, 1), :] = total[0:1, :]

    for k in range(3, 7):
        load[k].wait()
    by_block_production = exact(dual_resource_v[...], coef_production_v[...], ((1,), (1,)))
    by_block_setup = exact(dual_resource_v[...], coef_setup_v[...], ((1,), (1,)))
    stacked = jnp.concatenate(
        [t.astype(F32) for t in halves(by_block_production, 3) + halves(by_block_setup, 3)], axis=0
    ).astype(BF16)
    wide = 4

    @pl.loop(0, chunks // wide)
    def _(i):
        for k in range(wide):
            j = i * wide + k
            ids = jnp.broadcast_to(block_v[pl.ds(j, 1), :], (blocks, LANES))
            hot = ids == lax.broadcasted_iota(jnp.int32, (blocks, LANES), 0)
            onehot_v[:, lanes(j)] = jnp.where(hot, 1.0, 0.0).astype(BF16)
        at = pl.ds(pl.multiple_of(i * wide * LANES, wide * LANES), wide * LANES)
        pulled = jnp.dot(stacked, onehot_v[:, at], preferred_element_type=F32)
        pull_production_v[:, at] = pulled[0:rows] + (
            pulled[rows : 2 * rows] + pulled[2 * rows : 3 * rows]
        )
        pull_setup_v[:, at] = pulled[3 * rows : 4 * rows] + (
            pulled[4 * rows : 5 * rows] + pulled[5 * rows : 6 * rows]
        )

    for k in range(7, 16):
        load[k].wait()

    @pl.loop(0, chunks)
    def _(j):
        begin, stop, active = window(j)
        setup_price = row(cost_setup_v, j)
        late_price = row(penalty_v, j)
        for g in range(groups):
            on = active[g]
            dual_active = jnp.where(on, piece(dual_demand_v, g, j), 0.0)
            link_active = jnp.where(on, piece(dual_link_v, g, j), 0.0)
            primal_step = 1.0 / (2.0 + jnp.maximum(stop - period[g], 0.0))
            dual_step = 1.0 / (2.0 + jnp.maximum(period[g] - begin, 0.0))
            price = (
                piece(cost_production_v, g, j)
                - piece(local_v, g, j)
                + link_active
                + piece(pull_production_v, g, j)
            )
            put(local_v, g, j, piece(production_v, g, j) - primal_step * price)
            put(primal_step_v, g, j, primal_step)
            put(dual_step_v, g, j, dual_step)
            before = piece(setup_v, g, j)
            moved = jnp.clip(
                before - setup_step * (setup_price - big_m * link_active + piece(pull_setup_v, g, j)),
                0.0,
                1.0,
            )
            state = piece(fixing_v, g, j)
            moved = jnp.where(state == 1, 0.0, jnp.where(state == 2, 1.0, moved))
            moved = jnp.where(on, moved, 0.0)
            put(setup_v, g, j, moved)
            setup_bar = jnp.where(on, 2.0 * moved - before, 0.0)
            put(setup_bar_v, g, j, setup_bar)
            put(link_v, g, j, link_active - link_step * big_m * setup_bar)
            before = piece(shortage_v, g, j)
            late = jnp.where(
                on, jnp.maximum(before - short_step * (late_price - dual_active), 0.0), 0.0
            )
            put(shortage_v, g, j, late)
            put(dual_demand_v, g, j, dual_active - dual_step * (2.0 * late - before))

    stores = []

    def store(k, src, dst):
        copy = pltpu.make_async_copy(src, dst, out_sem.at[k])
        copy.start()
        stores.append(copy)

    store(0, setup_v, setup_o)
    store(1, shortage_v, shortage_o)

    pl.semaphore_wait(barrier, greeted)

    sent = []

    def remote(src, dst, send, recv, where):
        return pltpu.make_async_remote_copy(
            src_ref=src, dst_ref=dst, send_sem=send, recv_sem=recv, device_id=where, device_id_type=MESH
        )

    mine = pl.ds(pl.multiple_of(core * half, half), half)
    other = pl.ds(pl.multiple_of((1 - core) * half, half), half)

    def carried(s, later):
        def counts(there, here):
            return there > here if later else there < here

        sibling = place(x, z, 1 - core)
        to_core = remote(own_v.at[s], sibling_v.at[s], core_send.at[s], core_recv.at[s], sibling)
        to_core.start()
        sent.append(to_core)
        to_core.wait_recv()
        along_z_v[s, z] = own_v[s, mine, :] + sibling_v[s, mine, :]
        for d in sorted(range(1, nz), key=lambda d: -min(d, nz - d)):
            copy = remote(
                along_z_v.at[s, z],
                along_z_v.at[s, z],
                z_send.at[s, d],
                z_recv.at[s, z],
                place(x, lax.rem(z + d, nz), core),
            )
            copy.start()
            sent.append(copy)
        for d in range(1, nz):
            there = lax.rem(z + d, nz)
            remote(
                along_z_v.at[s, there],
                along_z_v.at[s, there],
                z_send.at[s, d],
                z_recv.at[s, there],
                place(x, there, core),
            ).wait_recv()
        whole = along_z_v[s, 0]
        partial = jnp.where(counts(0, z), whole, 0.0)
        for k in range(1, nz):
            term = along_z_v[s, k]
            whole = whole + term
            partial = partial + jnp.where(counts(k, z), term, 0.0)
        along_x_v[s, x, mine, :] = whole
        inside_v[s, mine, :] = partial
        for d in sorted(range(1, nx), key=lambda d: -min(d, nx - d)):
            for c in range(CORES):
                copy = remote(
                    along_x_v.at[s, x, mine],
                    along_x_v.at[s, x, mine],
                    x_send.at[s, d, c],
                    x_recv.at[s, x, core],
                    place(lax.rem(x + d, nx), z, c),
                )
                copy.start()
                sent.append(copy)
        to_core = remote(
            inside_v.at[s, mine], inside_v.at[s, mine], inside_send.at[s], inside_recv.at[s], sibling
        )
        to_core.start()
        sent.append(to_core)
        remote(
            inside_v.at[s, other], inside_v.at[s, other], inside_send.at[s], inside_recv.at[s], sibling
        ).wait_recv()
        total = inside_v[s] + jnp.where(counts(1 - core, core), sibling_v[s], 0.0)
        for d in range(1, nx):
            there = lax.rem(x + d, nx)
            for c in range(CORES):
                part = pl.ds(c * half, half)
                remote(
                    along_x_v.at[s, there, part],
                    along_x_v.at[s, there, part],
                    x_send.at[s, d, c],
                    x_recv.at[s, there, c],
                    place(there, z, c),
                ).wait_recv()
            total = total + jnp.where(counts(there, x), along_x_v[s, there], 0.0)
        carry_v[s] = total

    carried(0, True)

    @pl.loop(0, chunks)
    def _(j):
        begin, stop, active = window(j)
        carry = row(carry_v.at[0], j)
        total = jnp.zeros((GROUP, LANES), F32)
        for g in range(groups):
            on = active[g]
            before = piece(production_v, g, j)
            made = jnp.maximum(piece(local_v, g, j) + piece(primal_step_v, g, j) * carry, 0.0)
            made = jnp.where(on, made, 0.0)
            put(production_v, g, j, made)
            bar = jnp.where(on, 2.0 * made - before, 0.0)
            put(prod_bar_v, g, j, bar)
            flow = bar - jnp.where(on, piece(demand_v, g, j), 0.0)
            put(flow_v, g, j, flow)
            total = total + flow
        own_v[1, pl.ds(j, 1), :] = jnp.sum(total, axis=0, keepdims=True)

    store(2, production_v, production_o)

    @pl.loop(0, chunks)
    def _(j):
        begin, stop, active = window(j)
        heads = prefix_rows([piece(flow_v, g, j) for g in range(groups)], sub)
        for g in range(groups):
            put(
                dual_demand_v,
                g,
                j,
                piece(dual_demand_v, g, j) - piece(dual_step_v, g, j) * heads[g],
            )
            link = jnp.maximum(piece(link_v, g, j) + link_step * piece(prod_bar_v, g, j), 0.0)
            put(dual_link_v, g, j, jnp.where(active[g], link, 0.0))

    store(3, dual_link_v, dual_link_o)

    deep = DEPTH * LANES

    def add_blocks(i, total):
        at = pl.ds(pl.multiple_of(i * deep, deep), deep)
        terms = halves(prod_bar_v[:, at], 2) + halves(setup_bar_v[:, at], 2)
        left = jnp.concatenate(terms, axis=0)
        return total + lax.dot_general(
            left, onehot_v[:, at], (((1,), (1,)), ((), ())), preferred_element_type=F32
        )

    by_block = lax.fori_loop(0, items // deep, add_blocks, jnp.zeros((4 * rows, blocks), F32))
    usage_v[y] = exact(
        by_block[0:rows] + by_block[rows : 2 * rows], coef_production_v[...], ((1,), (0,))
    ) + exact(
        by_block[2 * rows : 3 * rows] + by_block[3 * rows : 4 * rows], coef_setup_v[...], ((1,), (0,))
    )
    for d in range(1, ny):
        copy = remote(
            usage_v.at[y], usage_v.at[y], y_send.at[d], y_recv.at[y], place(x, z, core, lax.rem(y + d, ny))
        )
        copy.start()
        sent.append(copy)

    carried(1, False)

    @pl.loop(0, chunks)
    def _(j):
        begin, stop, active = window(j)
        carry = row(carry_v.at[1], j)
        for g in range(groups):
            dual = piece(dual_demand_v, g, j) - piece(dual_step_v, g, j) * carry
            put(dual_demand_v, g, j, jnp.where(active[g], jnp.maximum(dual, 0.0), 0.0))

    store(4, dual_demand_v, dual_demand_o)

    for d in range(1, ny):
        there = lax.rem(y + d, ny)
        remote(
            usage_v.at[there], usage_v.at[there], y_send.at[d], y_recv.at[there], place(x, z, core, there)
        ).wait_recv()
    load[16].wait()
    usage = usage_v[0]
    for k in range(1, ny):
        usage = usage + usage_v[k]
    scale = dual_resource_v.shape[1] / items_total
    dual_resource_v[...] = jnp.maximum(dual_resource_v[...] + scale * (usage - capacity_v[...]), 0.0)
    store(5, dual_resource_v, dual_resource_o)

    for copy in stores:
        copy.wait()
    for copy in sent:
        copy.wait_send()


def shards(ranks, items_total, *args):
    (
        production,
        setup,
        shortage,
        dual_demand,
        dual_link,
        dual_resource,
        cost_production,
        cost_setup,
        penalty,
        demand,
        capacity,
        coef_production,
        coef_setup,
        horizon_start,
        horizon_end,
        fixing,
        block_id,
    ) = args
    nx, nz, ny = ranks
    rows, items = production.shape
    resources = dual_resource.shape[1]
    blocks = coef_production.shape[0]
    chunks = items // LANES
    per_item = (chunks, LANES)
    big, vector, small = (rows, items), (chunks, LANES), (rows, resources)

    def vmem(shape, dtype=F32):
        return pltpu.VMEM(shape, dtype)

    dma = pltpu.SemaphoreType.DMA
    anywhere = pl.BlockSpec(memory_space=pl.ANY)
    scratch = (
        [vmem(big)] * 7
        + [vmem(big, jnp.int32)]
        + [vmem(small)] * 2
        + [vmem((blocks, resources))] * 2
        + [vmem(vector)] * 2
        + [vmem(vector, jnp.int32)] * 3
        + [vmem(vector)] * 2
        + [vmem((blocks, items), BF16)]
        + [vmem(big)] * 9
        + [
            vmem((2,) + vector),
            vmem((2,) + vector),
            vmem((2, nz, chunks // 2, LANES)),
            vmem((2, nx) + vector),
            vmem((2,) + vector),
            vmem((2,) + vector),
            vmem((ny,) + small),
        ]
        + [
            dma((17,)),
            dma((6,)),
            dma((2,)),
            dma((2,)),
            dma((2, nz)),
            dma((2, nz)),
            dma((2, nx, CORES)),
            dma((2, nx, CORES)),
            dma((2,)),
            dma((2,)),
            dma((ny,)),
            dma((ny,)),
        ]
    )
    results = pl.pallas_call(
        functools.partial(kernel, ranks, items_total),
        out_shape=[jax.ShapeDtypeStruct(big, F32)] * 5 + [jax.ShapeDtypeStruct(small, F32)],
        in_specs=[pl.BlockSpec(memory_space=pltpu.HBM)] * 17,
        out_specs=[anywhere] * 6,
        scratch_shapes=scratch,
        compiler_params=pltpu.CompilerParams(
            collective_id=0, has_side_effects=True, vmem_limit_bytes=40 * 1024 * 1024
        ),
        name="lot_step",
    )(
        production,
        setup,
        shortage,
        dual_demand,
        dual_link,
        dual_resource,
        cost_production,
        cost_setup.reshape(per_item),
        penalty.reshape(per_item),
        demand,
        capacity,
        coef_production,
        coef_setup,
        horizon_start.reshape(per_item),
        horizon_end.reshape(per_item),
        fixing,
        block_id.reshape(per_item),
    )
    return tuple(results)


def solution(mesh):
    across, ny = mesh.shape["tm"], mesh.shape["items"]
    nz = 8
    nx = across // (nz * CORES)
    placed = (
        P("tm", "items"),
        P("tm", "items"),
        P("tm", "items"),
        P("tm", "items"),
        P("tm", "items"),
        P("tm", None),
        P("tm", "items"),
        P("items"),
        P("items"),
        P("tm", "items"),
        P("tm", None),
        P(),
        P(),
        P("items"),
        P("items"),
        P("tm", "items"),
        P("items"),
    )

    def step(*args):
        return jax.shard_map(
            functools.partial(shards, (nx, nz, ny), args[0].shape[1]),
            mesh=mesh,
            in_specs=placed,
            out_specs=(P("tm", "items"),) * 5 + (P("tm", None),),
            check_vma=False,
        )(*args)

    return step
```

```python
import functools

import jax
import jax.numpy as jnp
from jax import lax
from jax.experimental import pallas as pl
from jax.experimental.pallas import tpu as pltpu
from jax.sharding import PartitionSpec as P

MESH = pl.DeviceIdType.MESH
F32 = jnp.float32
BF16 = jnp.bfloat16

big_m = 4.0
setup_step = 0.5
short_step = 0.5
link_step = 0.25

LANES = 128
GROUP = 8
CORES = 2
DEPTH = 8


def suffix_rows(groups, sub):
    tail = jnp.zeros((GROUP, LANES), F32)
    out = [None] * len(groups)
    for g in reversed(range(len(groups))):
        part = groups[g]
        for shift in (1, 2, 4):
            moved = pltpu.roll(part, GROUP - shift, 0)
            part = part + jnp.where(sub < GROUP - shift, moved, 0.0)
        out[g] = part + tail
        tail = jnp.broadcast_to(out[g][0:1, :], (GROUP, LANES))
    return out, tail


def prefix_rows(groups, sub):
    head = jnp.zeros((GROUP, LANES), F32)
    out = [None] * len(groups)
    for g in range(len(groups)):
        part = groups[g]
        for shift in (1, 2, 4):
            moved = pltpu.roll(part, shift, 0)
            part = part + jnp.where(sub >= shift, moved, 0.0)
        out[g] = part + head
        head = jnp.broadcast_to(out[g][GROUP - 1 :, :], (GROUP, LANES))
    return out


def halves(value, count):
    terms = []
    for k in range(count):
        term = value.astype(BF16)
        terms.append(term)
        if k + 1 < count:
            value = value - term.astype(F32)
    return terms


def exact(left, right, contract):
    return lax.dot_general(
        left, right, (contract, ((), ())), precision=lax.Precision.HIGHEST, preferred_element_type=F32
    )


def kernel(
    ranks,
    items_total,
    production_h,
    setup_h,
    shortage_h,
    dual_demand_h,
    dual_link_h,
    dual_resource_h,
    cost_production_h,
    cost_setup_h,
    penalty_h,
    demand_h,
    capacity_h,
    coef_production_h,
    coef_setup_h,
    start_h,
    end_h,
    fixing_h,
    block_h,
    production_v,
    setup_v,
    shortage_v,
    dual_demand_v,
    dual_link_v,
    dual_resource_v,
    dual_step_v,
    window_v,
    cost_production_v,
    demand_v,
    fixing_v,
    capacity_v,
    coef_production_v,
    coef_setup_v,
    cost_setup_v,
    penalty_v,
    start_v,
    end_v,
    block_v,
    onehot_v,
    pull_production_v,
    pull_setup_v,
    local_v,
    primal_step_v,
    setup_bar_v,
    prod_bar_v,
    link_v,
    flow_v,
    own_v,
    sibling_v,
    along_z_v,
    along_x_v,
    inside_v,
    first_carry_v,
    usage_v,
    in_sem,
    core_send,
    core_recv,
    z_send,
    z_recv,
    x_send,
    x_recv,
    inside_send,
    inside_recv,
    y_send,
    y_recv,
):
    nx, nz, ny = ranks
    rows, items = production_v.shape
    groups = rows // GROUP
    chunks = items // LANES
    half = chunks // 2
    blocks = coef_production_v.shape[0]
    tm = lax.axis_index("tm")
    y = lax.axis_index("items")
    core = lax.rem(tm, CORES)
    z = lax.rem(tm // CORES, nz)
    x = tm // (CORES * nz)

    def place(px, pz, pc, py=None):
        return ((px * nz + pz) * CORES + pc, y if py is None else py)

    loads = {
        "start": (start_h, start_v),
        "end": (end_h, end_v),
        "dual_demand": (dual_demand_h, dual_demand_v),
        "block": (block_h, block_v),
        "dual_resource": (dual_resource_h, dual_resource_v),
        "coef_production": (coef_production_h, coef_production_v),
        "coef_setup": (coef_setup_h, coef_setup_v),
        "cost_setup": (cost_setup_h, cost_setup_v),
        "penalty": (penalty_h, penalty_v),
        "dual_link": (dual_link_h, dual_link_v),
        "setup": (setup_h, setup_v),
        "fixing": (fixing_h, fixing_v),
        "shortage": (shortage_h, shortage_v),
        "production": (production_h, production_v),
        "cost_production": (cost_production_h, cost_production_v),
        "demand": (demand_h, demand_v),
        "capacity": (capacity_h, capacity_v),
    }
    load = {
        name: pltpu.make_async_copy(src, dst, in_sem.at[k])
        for k, (name, (src, dst)) in enumerate(loads.items())
    }
    for copy in load.values():
        copy.start()

    def arrived(*names):
        for name in names:
            load[name].wait()

    barrier = pltpu.get_barrier_semaphore()
    greeted = 0
    for d in range(1, nz):
        pl.semaphore_signal(
            barrier, inc=1, device_id=place(x, lax.rem(z + d, nz), core), device_id_type=MESH
        )
        greeted += 1
    for d in range(1, nx):
        for c in range(CORES):
            pl.semaphore_signal(
                barrier, inc=1, device_id=place(lax.rem(x + d, nx), z, c), device_id_type=MESH
            )
            greeted += 1
    for d in range(1, ny):
        pl.semaphore_signal(
            barrier, inc=1, device_id=place(x, z, core, lax.rem(y + d, ny)), device_id_type=MESH
        )
        greeted += 1
    pl.semaphore_signal(barrier, inc=1, device_id=place(x, z, 1 - core), device_id_type=MESH)
    greeted += 1

    sub = lax.broadcasted_iota(jnp.int32, (GROUP, LANES), 0)
    first = (tm * rows).astype(F32)
    period = [sub.astype(F32) + (first + float(g * GROUP)) for g in range(groups)]

    def lanes(j):
        return pl.ds(pl.multiple_of(j * LANES, LANES), LANES)

    def piece(ref, g, j):
        return ref[g * GROUP : (g + 1) * GROUP, lanes(j)]

    def put(ref, g, j, value):
        ref[g * GROUP : (g + 1) * GROUP, lanes(j)] = value

    def row(ref, j):
        return jnp.broadcast_to(ref[pl.ds(j, 1), :], (GROUP, LANES))

    def window(j):
        begin, stop = row(window_v.at[0], j), row(window_v.at[1], j)
        return begin, stop, [(t >= begin) & (t <= stop) for t in period]

    arrived("start", "end")
    window_v[0] = start_v[...].astype(F32)
    window_v[1] = end_v[...].astype(F32)

    arrived("dual_demand")

    @pl.loop(0, chunks)
    def _(j):
        begin, stop, active = window(j)
        parts = [jnp.where(active[g], piece(dual_demand_v, g, j), 0.0) for g in range(groups)]
        tails, total = suffix_rows(parts, sub)
        for g in range(groups):
            put(local_v, g, j, tails[g])
        own_v[0, pl.ds(j, 1), :] = total[0:1, :]

    arrived("block", "dual_resource", "coef_production", "coef_setup")
    by_block_production = exact(dual_resource_v[...], coef_production_v[...], ((1,), (1,)))
    by_block_setup = exact(dual_resource_v[...], coef_setup_v[...], ((1,), (1,)))
    stacked = jnp.concatenate(
        [t.astype(F32) for t in halves(by_block_production, 3) + halves(by_block_setup, 3)], axis=0
    ).astype(BF16)
    wide = 4

    @pl.loop(0, chunks // wide)
    def _(i):
        for k in range(wide):
            j = i * wide + k
            ids = jnp.broadcast_to(block_v[pl.ds(j, 1), :], (blocks, LANES))
            hot = ids == lax.broadcasted_iota(jnp.int32, (blocks, LANES), 0)
            onehot_v[:, lanes(j)] = jnp.where(hot, 1.0, 0.0).astype(BF16)
        at = pl.ds(pl.multiple_of(i * wide * LANES, wide * LANES), wide * LANES)
        pulled = jnp.dot(stacked, onehot_v[:, at], preferred_element_type=F32)
        pull_production_v[:, at] = pulled[0:rows] + (
            pulled[rows : 2 * rows] + pulled[2 * rows : 3 * rows]
        )
        pull_setup_v[:, at] = pulled[3 * rows : 4 * rows] + (
            pulled[4 * rows : 5 * rows] + pulled[5 * rows : 6 * rows]
        )

    pl.semaphore_wait(barrier, greeted)

    sent = []

    def remote(src, dst, send, recv, where):
        return pltpu.make_async_remote_copy(
            src_ref=src, dst_ref=dst, send_sem=send, recv_sem=recv, device_id=where, device_id_type=MESH
        )

    mine = pl.ds(pl.multiple_of(core * half, half), half)
    other = pl.ds(pl.multiple_of((1 - core) * half, half), half)

    sibling = place(x, z, 1 - core)

    def halfway(s, h):
        part = pl.ds(pl.multiple_of(h * half, half), half)
        return remote(
            own_v.at[s, part], sibling_v.at[s, part], core_send.at[s, h], core_recv.at[s, h], sibling
        )

    def hand_over(s, h):
        copy = halfway(s, h)
        copy.start()
        sent.append(copy)

    def carried(s, later, during_z, during_x):
        def counts(there, here):
            return there > here if later else there < here

        halfway(s, core).wait_recv()
        along_z_v[s, z] = own_v[s, mine, :] + sibling_v[s, mine, :]
        for d in sorted(range(1, nz), key=lambda d: -min(d, nz - d)):
            copy = remote(
                along_z_v.at[s, z],
                along_z_v.at[s, z],
                z_send.at[s, d],
                z_recv.at[s, z],
                place(x, lax.rem(z + d, nz), core),
            )
            copy.start()
            sent.append(copy)
        during_z()
        for d in range(1, nz):
            there = lax.rem(z + d, nz)
            remote(
                along_z_v.at[s, there],
                along_z_v.at[s, there],
                z_send.at[s, d],
                z_recv.at[s, there],
                place(x, there, core),
            ).wait_recv()
        whole = along_z_v[s, 0]
        partial = jnp.where(counts(0, z), whole, 0.0)
        for k in range(1, nz):
            term = along_z_v[s, k]
            whole = whole + term
            partial = partial + jnp.where(counts(k, z), term, 0.0)
        along_x_v[s, x, mine, :] = whole
        inside_v[s, mine, :] = partial
        for d in sorted(range(1, nx), key=lambda d: -min(d, nx - d)):
            for c in range(CORES):
                copy = remote(
                    along_x_v.at[s, x, mine],
                    along_x_v.at[s, x, mine],
                    x_send.at[s, d, c],
                    x_recv.at[s, x, core],
                    place(lax.rem(x + d, nx), z, c),
                )
                copy.start()
                sent.append(copy)
        to_core = remote(
            inside_v.at[s, mine], inside_v.at[s, mine], inside_send.at[s], inside_recv.at[s], sibling
        )
        to_core.start()
        sent.append(to_core)
        during_x()
        halfway(s, 1 - core).wait_recv()
        remote(
            inside_v.at[s, other], inside_v.at[s, other], inside_send.at[s], inside_recv.at[s], sibling
        ).wait_recv()
        total = inside_v[s] + jnp.where(counts(1 - core, core), sibling_v[s], 0.0)
        for d in range(1, nx):
            there = lax.rem(x + d, nx)
            for c in range(CORES):
                part = pl.ds(c * half, half)
                remote(
                    along_x_v.at[s, there, part],
                    along_x_v.at[s, there, part],
                    x_send.at[s, d, c],
                    x_recv.at[s, there, c],
                    place(there, z, c),
                ).wait_recv()
            total = total + jnp.where(counts(there, x), along_x_v[s, there], 0.0)
        return total

    def own_part():
        arrived(
            "cost_setup",
            "penalty",
            "dual_link",
            "setup",
            "fixing",
            "shortage",
            "production",
            "cost_production",
        )

        @pl.loop(0, chunks)
        def _(j):
            begin, stop, active = window(j)
            setup_price = row(cost_setup_v, j)
            late_price = row(penalty_v, j)
            for g in range(groups):
                on = active[g]
                dual_active = jnp.where(on, piece(dual_demand_v, g, j), 0.0)
                link_active = jnp.where(on, piece(dual_link_v, g, j), 0.0)
                primal_step = 1.0 / (2.0 + jnp.maximum(stop - period[g], 0.0))
                dual_step = 1.0 / (2.0 + jnp.maximum(period[g] - begin, 0.0))
                price = (
                    piece(cost_production_v, g, j)
                    - piece(local_v, g, j)
                    + link_active
                    + piece(pull_production_v, g, j)
                )
                put(local_v, g, j, piece(production_v, g, j) - primal_step * price)
                put(primal_step_v, g, j, primal_step)
                put(dual_step_v, g, j, dual_step)
                before = piece(setup_v, g, j)
                moved = jnp.clip(
                    before - setup_step * (setup_price - big_m * link_active + piece(pull_setup_v, g, j)),
                    0.0,
                    1.0,
                )
                state = piece(fixing_v, g, j)
                moved = jnp.where(state == 1, 0.0, jnp.where(state == 2, 1.0, moved))
                moved = jnp.where(on, moved, 0.0)
                put(setup_v, g, j, moved)
                setup_bar = jnp.where(on, 2.0 * moved - before, 0.0)
                put(setup_bar_v, g, j, setup_bar)
                put(link_v, g, j, link_active - link_step * big_m * setup_bar)
                before = piece(shortage_v, g, j)
                late = jnp.where(
                    on, jnp.maximum(before - short_step * (late_price - dual_active), 0.0), 0.0
                )
                put(shortage_v, g, j, late)
                put(dual_demand_v, g, j, dual_active - dual_step * (2.0 * late - before))

    hand_over(0, 1 - core)
    hand_over(0, core)
    first_carry_v[...] = carried(0, True, own_part, lambda: None)

    arrived("demand")

    def net_production(j):
        begin, stop, active = window(j)
        carry = row(first_carry_v, j)
        total = jnp.zeros((GROUP, LANES), F32)
        for g in range(groups):
            on = active[g]
            before = piece(production_v, g, j)
            made = jnp.maximum(piece(local_v, g, j) + piece(primal_step_v, g, j) * carry, 0.0)
            made = jnp.where(on, made, 0.0)
            put(production_v, g, j, made)
            bar = jnp.where(on, 2.0 * made - before, 0.0)
            put(prod_bar_v, g, j, bar)
            flow = bar - jnp.where(on, piece(demand_v, g, j), 0.0)
            put(flow_v, g, j, flow)
            total = total + flow
        own_v[1, pl.ds(j, 1), :] = jnp.sum(total, axis=0, keepdims=True)

    for h in (1 - core, core):
        pl.loop(h * half, (h + 1) * half)(net_production)
        hand_over(1, h)

    def dual_part():
        @pl.loop(0, chunks)
        def _(j):
            begin, stop, active = window(j)
            heads = prefix_rows([piece(flow_v, g, j) for g in range(groups)], sub)
            for g in range(groups):
                put(
                    dual_demand_v,
                    g,
                    j,
                    piece(dual_demand_v, g, j) - piece(dual_step_v, g, j) * heads[g],
                )
                link = jnp.maximum(piece(link_v, g, j) + link_step * piece(prod_bar_v, g, j), 0.0)
                put(dual_link_v, g, j, jnp.where(active[g], link, 0.0))

        deep = DEPTH * LANES

        def add_blocks(i, total):
            at = pl.ds(pl.multiple_of(i * deep, deep), deep)
            terms = halves(prod_bar_v[:, at], 2) + halves(setup_bar_v[:, at], 2)
            left = jnp.concatenate(terms, axis=0)
            return total + lax.dot_general(
                left, onehot_v[:, at], (((1,), (1,)), ((), ())), preferred_element_type=F32
            )

        by_block = lax.fori_loop(0, items // deep, add_blocks, jnp.zeros((4 * rows, blocks), F32))
        usage_v[y] = exact(
            by_block[0:rows] + by_block[rows : 2 * rows], coef_production_v[...], ((1,), (0,))
        ) + exact(
            by_block[2 * rows : 3 * rows] + by_block[3 * rows : 4 * rows], coef_setup_v[...], ((1,), (0,))
        )
        for d in range(1, ny):
            copy = remote(
                usage_v.at[y], usage_v.at[y], y_send.at[d], y_recv.at[y], place(x, z, core, lax.rem(y + d, ny))
            )
            copy.start()
            sent.append(copy)

    def resource_part():
        for d in range(1, ny):
            there = lax.rem(y + d, ny)
            remote(
                usage_v.at[there], usage_v.at[there], y_send.at[d], y_recv.at[there], place(x, z, core, there)
            ).wait_recv()
        arrived("capacity")
        usage = usage_v[0]
        for k in range(1, ny):
            usage = usage + usage_v[k]
        scale = dual_resource_v.shape[1] / items_total
        dual_resource_v[...] = jnp.maximum(dual_resource_v[...] + scale * (usage - capacity_v[...]), 0.0)

    window_v[2] = carried(1, False, dual_part, resource_part)

    for copy in sent:
        copy.wait_send()


def finish(
    production_v,
    setup_v,
    shortage_v,
    dual_demand_v,
    dual_link_v,
    dual_resource_v,
    dual_step_v,
    window_v,
    production_o,
    setup_o,
    shortage_o,
    dual_demand_o,
    dual_link_o,
    dual_resource_o,
    result_v,
    out_sem,
):
    pairs = [
        (production_v, production_o),
        (setup_v, setup_o),
        (shortage_v, shortage_o),
        (dual_link_v, dual_link_o),
        (dual_resource_v, dual_resource_o),
    ]
    copies = [pltpu.make_async_copy(src, dst, out_sem.at[k]) for k, (src, dst) in enumerate(pairs)]
    for copy in copies:
        copy.start()
    rows, items = result_v.shape
    first = (lax.axis_index("tm") * rows).astype(F32)
    sub = lax.broadcasted_iota(jnp.int32, (GROUP, LANES), 0).astype(F32)

    @pl.loop(0, items // LANES)
    def _(j):
        at = pl.ds(pl.multiple_of(j * LANES, LANES), LANES)
        begin, stop, carry = [
            jnp.broadcast_to(window_v[k, pl.ds(j, 1), :], (GROUP, LANES)) for k in range(3)
        ]
        for g in range(rows // GROUP):
            t = sub + (first + float(g * GROUP))
            band = slice(g * GROUP, (g + 1) * GROUP)
            dual = jnp.maximum(dual_demand_v[band, at] - dual_step_v[band, at] * carry, 0.0)
            result_v[band, at] = jnp.where((t >= begin) & (t <= stop), dual, 0.0)

    last = pltpu.make_async_copy(result_v, dual_demand_o, out_sem.at[len(pairs)])
    last.start()
    for copy in copies:
        copy.wait()
    last.wait()


def shards(ranks, items_total, *args):
    (
        production,
        setup,
        shortage,
        dual_demand,
        dual_link,
        dual_resource,
        cost_production,
        cost_setup,
        penalty,
        demand,
        capacity,
        coef_production,
        coef_setup,
        horizon_start,
        horizon_end,
        fixing,
        block_id,
    ) = args
    nx, nz, ny = ranks
    rows, items = production.shape
    resources = dual_resource.shape[1]
    blocks = coef_production.shape[0]
    chunks = items // LANES
    per_item = (chunks, LANES)
    big, vector, small = (rows, items), (chunks, LANES), (rows, resources)

    def vmem(shape, dtype=F32):
        return pltpu.VMEM(shape, dtype)

    dma = pltpu.SemaphoreType.DMA
    anywhere = pl.BlockSpec(memory_space=pl.ANY)
    scratch = (
        [vmem(big)] * 2
        + [vmem(big, jnp.int32)]
        + [vmem(small)]
        + [vmem((blocks, resources))] * 2
        + [vmem(vector)] * 2
        + [vmem(vector, jnp.int32)] * 3
        + [vmem((blocks, items), BF16)]
        + [vmem(big)] * 8
        + [
            vmem((2,) + vector),
            vmem((2,) + vector),
            vmem((2, nz, chunks // 2, LANES)),
            vmem((2, nx) + vector),
            vmem((2,) + vector),
            vmem(vector),
            vmem((ny,) + small),
        ]
        + [
            dma((17,)),
            dma((2, CORES)),
            dma((2, CORES)),
            dma((2, nz)),
            dma((2, nz)),
            dma((2, nx, CORES)),
            dma((2, nx, CORES)),
            dma((2,)),
            dma((2,)),
            dma((ny,)),
            dma((ny,)),
        ]
    )
    operands = [
        production,
        setup,
        shortage,
        dual_demand,
        dual_link,
        dual_resource,
        cost_production,
        cost_setup.reshape(per_item),
        penalty.reshape(per_item),
        demand,
        capacity,
        coef_production,
        coef_setup,
        horizon_start.reshape(per_item),
        horizon_end.reshape(per_item),
        fixing,
        block_id.reshape(per_item),
    ]
    operands = [pltpu.with_memory_space_constraint(a, pltpu.HBM) for a in operands]
    held = pl.BlockSpec(memory_space=pltpu.VMEM)
    between = [big] * 5 + [small, big, (3,) + vector]
    parts = pl.pallas_call(
        functools.partial(kernel, ranks, items_total),
        out_shape=[pltpu.VMEM(shape, F32) for shape in between],
        in_specs=[anywhere] * 17,
        out_specs=[held] * len(between),
        scratch_shapes=scratch,
        compiler_params=pltpu.CompilerParams(
            collective_id=0, has_side_effects=True, vmem_limit_bytes=40 * 1024 * 1024
        ),
        name="lot_step",
    )(*operands)
    results = pl.pallas_call(
        finish,
        out_shape=[jax.ShapeDtypeStruct(big, F32)] * 5 + [jax.ShapeDtypeStruct(small, F32)],
        in_specs=[held] * len(between),
        out_specs=[anywhere] * 6,
        scratch_shapes=[vmem(big), dma((6,))],
        compiler_params=pltpu.CompilerParams(vmem_limit_bytes=8 * 1024 * 1024),
        name="finish",
    )(*parts)
    return tuple(results)


def solution(mesh):
    across, ny = mesh.shape["tm"], mesh.shape["items"]
    nz = 8
    nx = across // (nz * CORES)
    placed = (
        P("tm", "items"),
        P("tm", "items"),
        P("tm", "items"),
        P("tm", "items"),
        P("tm", "items"),
        P("tm", None),
        P("tm", "items"),
        P("items"),
        P("items"),
        P("tm", "items"),
        P("tm", None),
        P(),
        P(),
        P("items"),
        P("items"),
        P("tm", "items"),
        P("items"),
    )

    def step(*args):
        return jax.shard_map(
            functools.partial(shards, (nx, nz, ny), args[0].shape[1]),
            mesh=mesh,
            in_specs=placed,
            out_specs=(P("tm", "items"),) * 5 + (P("tm", None),),
            check_vma=False,
        )(*args)

    return step
```

```python
import functools

import jax
import jax.numpy as jnp
from jax import lax
from jax.experimental import pallas as pl
from jax.experimental.pallas import tpu as pltpu
from jax.sharding import PartitionSpec as P

MESH = pl.DeviceIdType.MESH
F32 = jnp.float32
BF16 = jnp.bfloat16

big_m = 4.0
setup_step = 0.5
short_step = 0.5
link_step = 0.25

LANES = 128
GROUP = 8
CORES = 2
DEPTH = 8
UNROLL = 4
PIECES = 4


def suffix_rows(groups, sub):
    tail = jnp.zeros((GROUP, LANES), F32)
    out = [None] * len(groups)
    for g in reversed(range(len(groups))):
        part = groups[g]
        for shift in (1, 2, 4):
            moved = pltpu.roll(part, GROUP - shift, 0)
            part = part + jnp.where(sub < GROUP - shift, moved, 0.0)
        out[g] = part + tail
        tail = jnp.broadcast_to(out[g][0:1, :], (GROUP, LANES))
    return out, tail


def prefix_rows(groups, sub):
    head = jnp.zeros((GROUP, LANES), F32)
    out = [None] * len(groups)
    for g in range(len(groups)):
        part = groups[g]
        for shift in (1, 2, 4):
            moved = pltpu.roll(part, shift, 0)
            part = part + jnp.where(sub >= shift, moved, 0.0)
        out[g] = part + head
        head = jnp.broadcast_to(out[g][GROUP - 1 :, :], (GROUP, LANES))
    return out


def halves(value, count):
    terms = []
    for k in range(count):
        term = value.astype(BF16)
        terms.append(term)
        if k + 1 < count:
            value = value - term.astype(F32)
    return terms


def far_first(count):
    return sorted(range(1, count), key=lambda d: -min(d, count - d))


def exact(left, right, contract):
    return lax.dot_general(
        left, right, (contract, ((), ())), precision=lax.Precision.HIGHEST, preferred_element_type=F32
    )


def kernel(
    ranks,
    items_total,
    production_h,
    setup_h,
    shortage_h,
    dual_demand_h,
    dual_link_h,
    dual_resource_h,
    cost_production_h,
    cost_setup_h,
    penalty_h,
    demand_h,
    capacity_h,
    coef_production_h,
    coef_setup_h,
    start_h,
    end_h,
    fixing_h,
    block_h,
    production_v,
    setup_v,
    shortage_v,
    dual_demand_v,
    dual_link_v,
    dual_resource_v,
    dual_step_v,
    window_v,
    cost_production_v,
    demand_v,
    fixing_v,
    capacity_v,
    coef_production_v,
    coef_setup_v,
    cost_setup_v,
    penalty_v,
    start_v,
    end_v,
    block_v,
    onehot_v,
    pull_production_v,
    pull_setup_v,
    local_v,
    primal_step_v,
    setup_bar_v,
    prod_bar_v,
    link_v,
    own_v,
    sibling_v,
    along_z_v,
    along_x_v,
    inside_v,
    carry_v,
    usage_v,
    in_sem,
    core_send,
    core_recv,
    z_send,
    z_recv,
    x_send,
    x_recv,
    inside_send,
    inside_recv,
    y_send,
    y_recv,
):
    nx, nz, ny = ranks
    rows, items = production_v.shape
    groups = rows // GROUP
    chunks = items // LANES
    half = chunks // 2
    blocks = coef_production_v.shape[0]
    tm = lax.axis_index("tm")
    y = lax.axis_index("items")
    core = lax.rem(tm, CORES)
    z = lax.rem(tm // CORES, nz)
    x = tm // (CORES * nz)

    def place(px, pz, pc, py=None):
        return ((px * nz + pz) * CORES + pc, y if py is None else py)

    barrier = pltpu.get_barrier_semaphore()
    greeted = 0
    for d in far_first(nz):
        pl.semaphore_signal(
            barrier, inc=1, device_id=place(x, lax.rem(z + d, nz), core), device_id_type=MESH
        )
        greeted += 1
    for d in far_first(nx):
        for c in range(CORES):
            pl.semaphore_signal(
                barrier, inc=1, device_id=place(lax.rem(x + d, nx), z, c), device_id_type=MESH
            )
            greeted += 1
    for d in range(1, ny):
        pl.semaphore_signal(
            barrier, inc=1, device_id=place(x, z, core, lax.rem(y + d, ny)), device_id_type=MESH
        )
        greeted += 1
    pl.semaphore_signal(barrier, inc=1, device_id=place(x, z, 1 - core), device_id_type=MESH)
    greeted += 1

    loads = {
        "start": (start_h, start_v),
        "end": (end_h, end_v),
        "dual_demand": (dual_demand_h, dual_demand_v),
        "block": (block_h, block_v),
        "dual_resource": (dual_resource_h, dual_resource_v),
        "coef_production": (coef_production_h, coef_production_v),
        "coef_setup": (coef_setup_h, coef_setup_v),
        "cost_setup": (cost_setup_h, cost_setup_v),
        "penalty": (penalty_h, penalty_v),
        "dual_link": (dual_link_h, dual_link_v),
        "setup": (setup_h, setup_v),
        "fixing": (fixing_h, fixing_v),
        "shortage": (shortage_h, shortage_v),
        "production": (production_h, production_v),
        "cost_production": (cost_production_h, cost_production_v),
        "demand": (demand_h, demand_v),
        "capacity": (capacity_h, capacity_v),
    }
    load = {
        name: pltpu.make_async_copy(src, dst, in_sem.at[k])
        for k, (name, (src, dst)) in enumerate(loads.items())
    }
    for copy in load.values():
        copy.start()

    def arrived(*names):
        for name in names:
            load[name].wait()

    sub = lax.broadcasted_iota(jnp.int32, (GROUP, LANES), 0)
    first = (tm * rows).astype(F32)
    period = [sub.astype(F32) + (first + float(g * GROUP)) for g in range(groups)]

    def lanes(j):
        return pl.ds(pl.multiple_of(j * LANES, LANES), LANES)

    def piece(ref, g, j):
        return ref[g * GROUP : (g + 1) * GROUP, lanes(j)]

    def put(ref, g, j, value):
        ref[g * GROUP : (g + 1) * GROUP, lanes(j)] = value

    def row(ref, j):
        return jnp.broadcast_to(ref[pl.ds(j, 1), :], (GROUP, LANES))

    def window(j):
        begin, stop = row(window_v.at[0], j), row(window_v.at[1], j)
        return begin, stop, [(t >= begin) & (t <= stop) for t in period]

    arrived("start", "end")
    window_v[0] = start_v[...].astype(F32)
    window_v[1] = end_v[...].astype(F32)

    arrived("dual_demand")

    @pl.loop(0, chunks)
    def _(j):
        begin, stop, active = window(j)
        parts = [jnp.where(active[g], piece(dual_demand_v, g, j), 0.0) for g in range(groups)]
        tails, total = suffix_rows(parts, sub)
        for g in range(groups):
            put(local_v, g, j, tails[g])
        own_v[0, pl.ds(j, 1), :] = total[0:1, :]

    pl.semaphore_wait(barrier, greeted)

    sent = []

    def remote(src, dst, send, recv, where):
        return pltpu.make_async_remote_copy(
            src_ref=src, dst_ref=dst, send_sem=send, recv_sem=recv, device_id=where, device_id_type=MESH
        )

    mine = pl.ds(pl.multiple_of(core * half, half), half)
    other = pl.ds(pl.multiple_of((1 - core) * half, half), half)

    sibling = place(x, z, 1 - core)

    def halfway(s, h):
        part = pl.ds(pl.multiple_of(h * half, half), half)
        return remote(
            own_v.at[s, part], sibling_v.at[s, part], core_send.at[s, h], core_recv.at[s, h], sibling
        )

    def hand_over(s, h):
        copy = halfway(s, h)
        copy.start()
        sent.append(copy)

    def across(s, d, c):
        return remote(
            along_x_v.at[s, x, mine],
            along_x_v.at[s, x, mine],
            x_send.at[s, d, c],
            x_recv.at[s, x, core],
            place(lax.rem(x + d, nx), z, c),
        )

    def carried(s, later, during_z, during_x):
        def counts(there, here):
            return there > here if later else there < here

        halfway(s, core).wait_recv()
        along_z_v[s, z] = own_v[s, mine, :] + sibling_v[s, mine, :]
        for d in far_first(nz):
            copy = remote(
                along_z_v.at[s, z],
                along_z_v.at[s, z],
                z_send.at[s, d],
                z_recv.at[s, z],
                place(x, lax.rem(z + d, nz), core),
            )
            copy.start()
            sent.append(copy)
        during_z()
        for d in range(1, nz):
            there = lax.rem(z + d, nz)
            remote(
                along_z_v.at[s, there],
                along_z_v.at[s, there],
                z_send.at[s, d],
                z_recv.at[s, there],
                place(x, there, core),
            ).wait_recv()
        whole = along_z_v[s, 0]
        partial = jnp.where(counts(0, z), whole, 0.0)
        for k in range(1, nz):
            term = along_z_v[s, k]
            whole = whole + term
            partial = partial + jnp.where(counts(k, z), term, 0.0)
        along_x_v[s, x, mine, :] = whole
        inside_v[s, mine, :] = partial
        for d in far_first(nx):
            there = lax.rem(x + d, nx)

            @pl.when(counts(x, there))
            def _():
                for c in range(CORES):
                    across(s, d, c).start()

        to_core = remote(
            inside_v.at[s, mine], inside_v.at[s, mine], inside_send.at[s], inside_recv.at[s], sibling
        )
        to_core.start()
        sent.append(to_core)
        during_x()
        halfway(s, 1 - core).wait_recv()
        remote(
            inside_v.at[s, other], inside_v.at[s, other], inside_send.at[s], inside_recv.at[s], sibling
        ).wait_recv()
        carry_v[s] = inside_v[s] + jnp.where(counts(1 - core, core), sibling_v[s], 0.0)
        for d in reversed(far_first(nx)):
            there = lax.rem(x + d, nx)

            @pl.when(counts(there, x))
            def _():
                for c in range(CORES):
                    part = pl.ds(c * half, half)
                    remote(
                        along_x_v.at[s, there, part],
                        along_x_v.at[s, there, part],
                        x_send.at[s, d, c],
                        x_recv.at[s, there, c],
                        place(there, z, c),
                    ).wait_recv()
                carry_v[s] += along_x_v[s, there]

    def left(s, later):
        for copy in sent:
            copy.wait_send()
        sent.clear()
        for d in far_first(nx):
            there = lax.rem(x + d, nx)

            @pl.when(x > there if later else x < there)
            def _():
                for c in range(CORES):
                    across(s, d, c).wait_send()

    def pull():
        arrived("block", "dual_resource", "coef_production", "coef_setup")
        by_block_production = exact(dual_resource_v[...], coef_production_v[...], ((1,), (1,)))
        by_block_setup = exact(dual_resource_v[...], coef_setup_v[...], ((1,), (1,)))
        stacked = jnp.concatenate(
            [t.astype(F32) for t in halves(by_block_production, 3) + halves(by_block_setup, 3)], axis=0
        ).astype(BF16)
        wide = 4

        @pl.loop(0, chunks // wide)
        def _(i):
            for k in range(wide):
                j = i * wide + k
                ids = jnp.broadcast_to(block_v[pl.ds(j, 1), :], (blocks, LANES))
                hot = ids == lax.broadcasted_iota(jnp.int32, (blocks, LANES), 0)
                onehot_v[:, lanes(j)] = jnp.where(hot, 1.0, 0.0).astype(BF16)
            at = pl.ds(pl.multiple_of(i * wide * LANES, wide * LANES), wide * LANES)
            pulled = jnp.dot(stacked, onehot_v[:, at], preferred_element_type=F32)
            pull_production_v[:, at] = pulled[0:rows] + (
                pulled[rows : 2 * rows] + pulled[2 * rows : 3 * rows]
            )
            pull_setup_v[:, at] = pulled[3 * rows : 4 * rows] + (
                pulled[4 * rows : 5 * rows] + pulled[5 * rows : 6 * rows]
            )

    def own_part():
        arrived(
            "cost_setup",
            "penalty",
            "dual_link",
            "setup",
            "fixing",
            "shortage",
            "production",
            "cost_production",
        )

        @pl.loop(0, chunks)
        def _(j):
            begin, stop, active = window(j)
            setup_price = row(cost_setup_v, j)
            late_price = row(penalty_v, j)
            for g in range(groups):
                on = active[g]
                dual_active = jnp.where(on, piece(dual_demand_v, g, j), 0.0)
                link_active = jnp.where(on, piece(dual_link_v, g, j), 0.0)
                primal_step = 1.0 / (2.0 + jnp.maximum(stop - period[g], 0.0))
                dual_step = 1.0 / (2.0 + jnp.maximum(period[g] - begin, 0.0))
                price = (
                    piece(cost_production_v, g, j)
                    - piece(local_v, g, j)
                    + link_active
                    + piece(pull_production_v, g, j)
                )
                put(local_v, g, j, piece(production_v, g, j) - primal_step * price)
                put(primal_step_v, g, j, primal_step)
                put(dual_step_v, g, j, dual_step)
                before = piece(setup_v, g, j)
                moved = jnp.clip(
                    before - setup_step * (setup_price - big_m * link_active + piece(pull_setup_v, g, j)),
                    0.0,
                    1.0,
                )
                state = piece(fixing_v, g, j)
                moved = jnp.where(state == 1, 0.0, jnp.where(state == 2, 1.0, moved))
                moved = jnp.where(on, moved, 0.0)
                put(setup_v, g, j, moved)
                setup_bar = jnp.where(on, 2.0 * moved - before, 0.0)
                put(setup_bar_v, g, j, setup_bar)
                put(link_v, g, j, link_active - link_step * big_m * setup_bar)
                before = piece(shortage_v, g, j)
                late = jnp.where(
                    on, jnp.maximum(before - short_step * (late_price - dual_active), 0.0), 0.0
                )
                put(shortage_v, g, j, late)
                put(dual_demand_v, g, j, dual_active - dual_step * (2.0 * late - before))

    hand_over(0, 1 - core)
    hand_over(0, core)
    carried(0, True, pull, own_part)

    arrived("demand")

    def net_production(j):
        begin, stop, active = window(j)
        carry = row(carry_v.at[0], j)
        total = jnp.zeros((GROUP, LANES), F32)
        for g in range(groups):
            on = active[g]
            before = piece(production_v, g, j)
            made = jnp.maximum(piece(local_v, g, j) + piece(primal_step_v, g, j) * carry, 0.0)
            made = jnp.where(on, made, 0.0)
            put(production_v, g, j, made)
            bar = jnp.where(on, 2.0 * made - before, 0.0)
            put(prod_bar_v, g, j, bar)
            total = total + (bar - jnp.where(on, piece(demand_v, g, j), 0.0))
        own_v[1, pl.ds(j, 1), :] = jnp.sum(total, axis=0, keepdims=True)

    for h in (1 - core, core):

        @pl.loop(0, half // UNROLL)
        def _(i):
            for k in range(UNROLL):
                net_production(h * half + i * UNROLL + k)

        hand_over(1, h)

    def dual_part():
        @pl.loop(0, chunks)
        def _(j):
            begin, stop, active = window(j)
            flow = [
                piece(prod_bar_v, g, j) - jnp.where(active[g], piece(demand_v, g, j), 0.0)
                for g in range(groups)
            ]
            heads = prefix_rows(flow, sub)
            for g in range(groups):
                put(
                    dual_demand_v,
                    g,
                    j,
                    piece(dual_demand_v, g, j) - piece(dual_step_v, g, j) * heads[g],
                )
                link = jnp.maximum(piece(link_v, g, j) + link_step * piece(prod_bar_v, g, j), 0.0)
                put(dual_link_v, g, j, jnp.where(active[g], link, 0.0))

        deep = DEPTH * LANES

        def add_blocks(i, total):
            at = pl.ds(pl.multiple_of(i * deep, deep), deep)
            terms = halves(prod_bar_v[:, at], 2) + halves(setup_bar_v[:, at], 2)
            left = jnp.concatenate(terms, axis=0)
            return total + lax.dot_general(
                left, onehot_v[:, at], (((1,), (1,)), ((), ())), preferred_element_type=F32
            )

        by_block = lax.fori_loop(0, items // deep, add_blocks, jnp.zeros((4 * rows, blocks), F32))
        usage_v[y] = exact(
            by_block[0:rows] + by_block[rows : 2 * rows], coef_production_v[...], ((1,), (0,))
        ) + exact(
            by_block[2 * rows : 3 * rows] + by_block[3 * rows : 4 * rows], coef_setup_v[...], ((1,), (0,))
        )
        for d in range(1, ny):
            copy = remote(
                usage_v.at[y], usage_v.at[y], y_send.at[d], y_recv.at[y], place(x, z, core, lax.rem(y + d, ny))
            )
            copy.start()
            sent.append(copy)

    def resource_part():
        for d in range(1, ny):
            there = lax.rem(y + d, ny)
            remote(
                usage_v.at[there], usage_v.at[there], y_send.at[d], y_recv.at[there], place(x, z, core, there)
            ).wait_recv()
        arrived("capacity")
        usage = usage_v[0]
        for k in range(1, ny):
            usage = usage + usage_v[k]
        scale = dual_resource_v.shape[1] / items_total
        dual_resource_v[...] = jnp.maximum(dual_resource_v[...] + scale * (usage - capacity_v[...]), 0.0)

    def rest():
        resource_part()
        left(0, True)

    carried(1, False, dual_part, rest)
    window_v[2] = carry_v[1]
    left(1, False)


def finish(
    production_v,
    setup_v,
    shortage_v,
    dual_demand_v,
    dual_link_v,
    dual_resource_v,
    dual_step_v,
    window_v,
    production_o,
    setup_o,
    shortage_o,
    dual_demand_o,
    dual_link_o,
    dual_resource_o,
    result_v,
    out_sem,
):
    pairs = [
        (production_v, production_o),
        (setup_v, setup_o),
        (shortage_v, shortage_o),
        (dual_link_v, dual_link_o),
        (dual_resource_v, dual_resource_o),
    ]
    copies = [pltpu.make_async_copy(src, dst, out_sem.at[k]) for k, (src, dst) in enumerate(pairs)]
    for copy in copies:
        copy.start()
    rows, items = result_v.shape
    first = (lax.axis_index("tm") * rows).astype(F32)
    sub = lax.broadcasted_iota(jnp.int32, (GROUP, LANES), 0).astype(F32)

    step = items // PIECES
    for p in range(PIECES):

        @pl.loop(p * step // LANES, (p + 1) * step // LANES, step=2)
        def _(i):
            for j in (i, i + 1):
                at = pl.ds(pl.multiple_of(j * LANES, LANES), LANES)
                begin, stop, carry = [
                    jnp.broadcast_to(window_v[k, pl.ds(j, 1), :], (GROUP, LANES)) for k in range(3)
                ]
                for g in range(rows // GROUP):
                    t = sub + (first + float(g * GROUP))
                    band = slice(g * GROUP, (g + 1) * GROUP)
                    dual = jnp.maximum(dual_demand_v[band, at] - dual_step_v[band, at] * carry, 0.0)
                    result_v[band, at] = jnp.where((t >= begin) & (t <= stop), dual, 0.0)

        at = pl.ds(p * step, step)
        copies.append(
            pltpu.make_async_copy(result_v.at[:, at], dual_demand_o.at[:, at], out_sem.at[len(pairs) + p])
        )
        copies[-1].start()

    for copy in copies:
        copy.wait()


def shards(ranks, items_total, *args):
    (
        production,
        setup,
        shortage,
        dual_demand,
        dual_link,
        dual_resource,
        cost_production,
        cost_setup,
        penalty,
        demand,
        capacity,
        coef_production,
        coef_setup,
        horizon_start,
        horizon_end,
        fixing,
        block_id,
    ) = args
    nx, nz, ny = ranks
    rows, items = production.shape
    resources = dual_resource.shape[1]
    blocks = coef_production.shape[0]
    chunks = items // LANES
    per_item = (chunks, LANES)
    big, vector, small = (rows, items), (chunks, LANES), (rows, resources)

    def vmem(shape, dtype=F32):
        return pltpu.VMEM(shape, dtype)

    dma = pltpu.SemaphoreType.DMA
    anywhere = pl.BlockSpec(memory_space=pl.ANY)
    scratch = (
        [vmem(big)] * 2
        + [vmem(big, jnp.int32)]
        + [vmem(small)]
        + [vmem((blocks, resources))] * 2
        + [vmem(vector)] * 2
        + [vmem(vector, jnp.int32)] * 3
        + [vmem((blocks, items), BF16)]
        + [vmem(big)] * 7
        + [
            vmem((2,) + vector),
            vmem((2,) + vector),
            vmem((2, nz, chunks // 2, LANES)),
            vmem((2, nx) + vector),
            vmem((2,) + vector),
            vmem((2,) + vector),
            vmem((ny,) + small),
        ]
        + [
            dma((17,)),
            dma((2, CORES)),
            dma((2, CORES)),
            dma((2, nz)),
            dma((2, nz)),
            dma((2, nx, CORES)),
            dma((2, nx, CORES)),
            dma((2,)),
            dma((2,)),
            dma((ny,)),
            dma((ny,)),
        ]
    )
    operands = [
        production,
        setup,
        shortage,
        dual_demand,
        dual_link,
        dual_resource,
        cost_production,
        cost_setup.reshape(per_item),
        penalty.reshape(per_item),
        demand,
        capacity,
        coef_production,
        coef_setup,
        horizon_start.reshape(per_item),
        horizon_end.reshape(per_item),
        fixing,
        block_id.reshape(per_item),
    ]
    operands = [pltpu.with_memory_space_constraint(a, pltpu.HBM) for a in operands]
    held = pl.BlockSpec(memory_space=pltpu.VMEM)
    between = [big] * 5 + [small, big, (3,) + vector]
    parts = pl.pallas_call(
        functools.partial(kernel, ranks, items_total),
        out_shape=[pltpu.VMEM(shape, F32) for shape in between],
        in_specs=[anywhere] * 17,
        out_specs=[held] * len(between),
        scratch_shapes=scratch,
        compiler_params=pltpu.CompilerParams(
            collective_id=0, has_side_effects=True, vmem_limit_bytes=40 * 1024 * 1024
        ),
        name="lot_step",
    )(*operands)
    results = pl.pallas_call(
        finish,
        out_shape=[jax.ShapeDtypeStruct(big, F32)] * 5 + [jax.ShapeDtypeStruct(small, F32)],
        in_specs=[held] * len(between),
        out_specs=[anywhere] * 6,
        scratch_shapes=[vmem(big), dma((5 + PIECES,))],
        compiler_params=pltpu.CompilerParams(vmem_limit_bytes=8 * 1024 * 1024),
        name="finish",
    )(*parts)
    return tuple(results)


def solution(mesh):
    across, ny = mesh.shape["tm"], mesh.shape["items"]
    nz = 8
    nx = across // (nz * CORES)
    placed = (
        P("tm", "items"),
        P("tm", "items"),
        P("tm", "items"),
        P("tm", "items"),
        P("tm", "items"),
        P("tm", None),
        P("tm", "items"),
        P("items"),
        P("items"),
        P("tm", "items"),
        P("tm", None),
        P(),
        P(),
        P("items"),
        P("items"),
        P("tm", "items"),
        P("items"),
    )

    def step(*args):
        return jax.shard_map(
            functools.partial(shards, (nx, nz, ny), args[0].shape[1]),
            mesh=mesh,
            in_specs=placed,
            out_specs=(P("tm", "items"),) * 5 + (P("tm", None),),
            check_vma=False,
        )(*args)

    return step
```

```python
import functools

import jax
import jax.numpy as jnp
from jax import lax
from jax.experimental import pallas as pl
from jax.experimental.pallas import tpu as pltpu
from jax.sharding import PartitionSpec as P

MESH = pl.DeviceIdType.MESH
F32 = jnp.float32
BF16 = jnp.bfloat16

big_m = 4.0
setup_step = 0.5
short_step = 0.5
link_step = 0.25

LANES = 128
GROUP = 8
CORES = 2
DEPTH = 8
UNROLL = 4
RELAY = 2
PIECES = 4


def suffix_rows(groups, sub):
    tail = jnp.zeros((GROUP, LANES), F32)
    out = [None] * len(groups)
    for g in reversed(range(len(groups))):
        part = groups[g]
        for shift in (1, 2, 4):
            moved = pltpu.roll(part, GROUP - shift, 0)
            part = part + jnp.where(sub < GROUP - shift, moved, 0.0)
        out[g] = part + tail
        tail = jnp.broadcast_to(out[g][0:1, :], (GROUP, LANES))
    return out, tail


def prefix_rows(groups, sub):
    head = jnp.zeros((GROUP, LANES), F32)
    out = [None] * len(groups)
    for g in range(len(groups)):
        part = groups[g]
        for shift in (1, 2, 4):
            moved = pltpu.roll(part, shift, 0)
            part = part + jnp.where(sub >= shift, moved, 0.0)
        out[g] = part + head
        head = jnp.broadcast_to(out[g][GROUP - 1 :, :], (GROUP, LANES))
    return out


def halves(value, count):
    terms = []
    for k in range(count):
        term = value.astype(BF16)
        terms.append(term)
        if k + 1 < count:
            value = value - term.astype(F32)
    return terms


def far_first(count):
    return sorted(range(1, count), key=lambda d: -min(d, count - d))


def exact(left, right, contract):
    return lax.dot_general(
        left, right, (contract, ((), ())), precision=lax.Precision.HIGHEST, preferred_element_type=F32
    )


def kernel(
    ranks,
    items_total,
    production_h,
    setup_h,
    shortage_h,
    dual_demand_h,
    dual_link_h,
    dual_resource_h,
    cost_production_h,
    cost_setup_h,
    penalty_h,
    demand_h,
    capacity_h,
    coef_production_h,
    coef_setup_h,
    start_h,
    end_h,
    fixing_h,
    block_h,
    production_v,
    setup_v,
    shortage_v,
    dual_demand_v,
    dual_link_v,
    dual_resource_v,
    dual_step_v,
    window_v,
    cost_production_v,
    demand_v,
    fixing_v,
    capacity_v,
    coef_production_v,
    coef_setup_v,
    cost_setup_v,
    penalty_v,
    start_v,
    end_v,
    block_v,
    onehot_v,
    pull_production_v,
    pull_setup_v,
    local_v,
    primal_step_v,
    setup_bar_v,
    prod_bar_v,
    link_v,
    own_v,
    sibling_v,
    along_z_v,
    along_x_v,
    inside_v,
    raw_x_v,
    column_v,
    usage_v,
    in_sem,
    core_send,
    core_recv,
    z_send,
    z_recv,
    x_send,
    x_recv,
    inside_send,
    inside_recv,
    raw_send,
    raw_recv,
    ready,
    y_send,
    y_recv,
):
    nx, nz, ny = ranks
    rows, items = production_v.shape
    groups = rows // GROUP
    chunks = items // LANES
    half = chunks // 2
    blocks = coef_production_v.shape[0]
    tm = lax.axis_index("tm")
    y = lax.axis_index("items")
    core = lax.rem(tm, CORES)
    z = lax.rem(tm // CORES, nz)
    x = tm // (CORES * nz)

    def place(px, pz, pc, py=None):
        return ((px * nz + pz) * CORES + pc, y if py is None else py)

    barrier = pltpu.get_barrier_semaphore()
    greeted = 0
    for d in [d for d in far_first(nz) if min(d, nz - d) <= RELAY]:
        pl.semaphore_signal(
            barrier, inc=1, device_id=place(x, lax.rem(z + d, nz), core), device_id_type=MESH
        )
        greeted += 1
    for d in far_first(nx):
        for c in range(CORES):
            pl.semaphore_signal(
                barrier, inc=1, device_id=place(lax.rem(x + d, nx), z, c), device_id_type=MESH
            )
            greeted += 1
    for d in range(1, ny):
        pl.semaphore_signal(
            barrier, inc=1, device_id=place(x, z, core, lax.rem(y + d, ny)), device_id_type=MESH
        )
        greeted += 1
    pl.semaphore_signal(barrier, inc=1, device_id=place(x, z, 1 - core), device_id_type=MESH)
    greeted += 1

    loads = {
        "start": (start_h, start_v),
        "end": (end_h, end_v),
        "dual_demand": (dual_demand_h, dual_demand_v),
        "block": (block_h, block_v),
        "dual_resource": (dual_resource_h, dual_resource_v),
        "coef_production": (coef_production_h, coef_production_v),
        "coef_setup": (coef_setup_h, coef_setup_v),
        "cost_setup": (cost_setup_h, cost_setup_v),
        "penalty": (penalty_h, penalty_v),
        "dual_link": (dual_link_h, dual_link_v),
        "setup": (setup_h, setup_v),
        "fixing": (fixing_h, fixing_v),
        "shortage": (shortage_h, shortage_v),
        "production": (production_h, production_v),
        "cost_production": (cost_production_h, cost_production_v),
        "demand": (demand_h, demand_v),
        "capacity": (capacity_h, capacity_v),
    }
    load = {
        name: pltpu.make_async_copy(src, dst, in_sem.at[k])
        for k, (name, (src, dst)) in enumerate(loads.items())
    }
    for copy in load.values():
        copy.start()

    def arrived(*names):
        for name in names:
            load[name].wait()

    sub = lax.broadcasted_iota(jnp.int32, (GROUP, LANES), 0)
    first = (tm * rows).astype(F32)
    period = [sub.astype(F32) + (first + float(g * GROUP)) for g in range(groups)]

    def lanes(j):
        return pl.ds(pl.multiple_of(j * LANES, LANES), LANES)

    def piece(ref, g, j):
        return ref[g * GROUP : (g + 1) * GROUP, lanes(j)]

    def put(ref, g, j, value):
        ref[g * GROUP : (g + 1) * GROUP, lanes(j)] = value

    def row(ref, j):
        return jnp.broadcast_to(ref[pl.ds(j, 1), :], (GROUP, LANES))

    def window(j):
        begin, stop = row(window_v.at[0], j), row(window_v.at[1], j)
        return begin, stop, [(t >= begin) & (t <= stop) for t in period]

    arrived("start", "end")
    window_v[0] = start_v[...].astype(F32)
    window_v[1] = end_v[...].astype(F32)

    arrived("dual_demand")

    @pl.loop(0, chunks)
    def _(j):
        begin, stop, active = window(j)
        parts = [jnp.where(active[g], piece(dual_demand_v, g, j), 0.0) for g in range(groups)]
        tails, total = suffix_rows(parts, sub)
        for g in range(groups):
            put(local_v, g, j, tails[g])
        own_v[0, pl.ds(j, 1), :] = total[0:1, :]

    pl.semaphore_wait(barrier, greeted)

    def remote(src, dst, send, recv, where):
        return pltpu.make_async_remote_copy(
            src_ref=src, dst_ref=dst, send_sem=send, recv_sem=recv, device_id=where, device_id_type=MESH
        )

    def part(h):
        return pl.ds(pl.multiple_of(h * half, half), half)

    sibling = place(x, z, 1 - core)
    mine, other = part(core), part(1 - core)

    def halfway(s, h):
        return remote(
            own_v.at[s, part(h)], sibling_v.at[s, part(h)], core_send.at[s, h], core_recv.at[s, h], sibling
        )

    def along(s, src, e):
        return remote(
            src, along_z_v.at[s, z], z_send.at[s, e], z_recv.at[s, z], place(x, lax.rem(z + e, nz), core)
        )

    def from_along(s, e):
        there = lax.rem(z + e, nz)
        remote(
            along_z_v.at[s, there],
            along_z_v.at[s, there],
            z_send.at[s, e],
            z_recv.at[s, there],
            place(x, there, core),
        ).wait_recv()
        return along_z_v[s, there]

    def raw(d, c):
        return remote(
            own_v.at[0, part(c)],
            raw_x_v.at[x, core],
            raw_send.at[d, c],
            raw_recv.at[x, core],
            place(lax.rem(x + d, nx), z, c),
        )

    def across(d, c):
        return remote(
            along_x_v.at[x, other],
            along_x_v.at[x, other],
            x_send.at[d, c],
            x_recv.at[x, 1 - core],
            place(lax.rem(x + d, nx), z, c),
        )

    def inside(s, where):
        return remote(
            inside_v.at[s, where], inside_v.at[s, where], inside_send.at[s], inside_recv.at[s], sibling
        )

    def column(e):
        there = lax.rem(z + e, nz)
        return along(0, column_v.at[jnp.where(z > there, 1, 0)], e)

    later_core = core == 0

    def suffix_scan(during_x, during_z):
        for d in far_first(nx):

            @pl.when(x > lax.rem(x + d, nx))
            def _():
                for c in range(CORES):
                    raw(d, c).start()

        halfway(0, 1 - core).start()
        halfway(0, core).start()
        for e in (RELAY, nz - RELAY):
            pl.semaphore_signal(
                ready, inc=1, device_id=place(x, lax.rem(z + e, nz), core), device_id_type=MESH
            )
        during_x()
        halfway(0, core).wait_recv()
        column_v[0] = jnp.zeros((half, LANES), F32)
        for d in reversed(far_first(nx)):
            there = lax.rem(x + d, nx)

            @pl.when(there > x)
            def _():
                for c in range(CORES):
                    remote(
                        raw_x_v.at[there, c],
                        raw_x_v.at[there, c],
                        raw_send.at[d, c],
                        raw_recv.at[there, c],
                        place(there, z, c),
                    ).wait_recv()
                column_v[0] += raw_x_v[there, 0] + raw_x_v[there, 1]

        column_v[1] = column_v[0] + (own_v[0, mine, :] + sibling_v[0, mine, :])
        pl.semaphore_wait(ready, 2)
        for e in far_first(nz):
            column(e).start()
        during_z()
        total = column_v[0]
        for e in reversed(far_first(nz)):
            total = total + from_along(0, e)
        inside_v[0, mine, :] = total
        inside(0, mine).start()
        window_v[2, mine, :] = total + jnp.where(later_core, sibling_v[0, mine, :], 0.0)

    def suffix_other():
        halfway(0, 1 - core).wait_recv()
        inside(0, other).wait_recv()
        window_v[2, other, :] = inside_v[0, other, :] + jnp.where(
            later_core, sibling_v[0, other, :], 0.0
        )

    def suffix_left():
        for d in far_first(nx):

            @pl.when(x > lax.rem(x + d, nx))
            def _():
                for c in range(CORES):
                    raw(d, c).wait_send()

        for h in range(CORES):
            halfway(0, h).wait_send()
        for e in far_first(nz):
            column(e).wait_send()
        inside(0, mine).wait_send()

    def prefix_scan(during_z, during_x):
        halfway(1, 1 - core).wait_recv()
        along_z_v[1, z] = own_v[1, other, :] + sibling_v[1, other, :]
        for e in far_first(nz):
            along(1, along_z_v.at[1, z], e).start()
        during_z()
        whole = along_z_v[1, z]
        partial = jnp.zeros_like(whole)
        for e in reversed(far_first(nz)):
            term = from_along(1, e)
            whole = whole + term
            partial = partial + jnp.where(lax.rem(z + e, nz) < z, term, 0.0)
        along_x_v[x, other, :] = whole
        for d in far_first(nx):

            @pl.when(x < lax.rem(x + d, nx))
            def _():
                for c in range(CORES):
                    across(d, c).start()

        inside_v[1, other, :] = partial
        inside(1, other).start()
        during_x()
        halfway(1, core).wait_recv()
        inside(1, mine).wait_recv()
        window_v[3] = inside_v[1] + jnp.where(later_core, 0.0, sibling_v[1])
        for d in reversed(far_first(nx)):
            there = lax.rem(x + d, nx)

            @pl.when(there < x)
            def _():
                for h in range(CORES):
                    remote(
                        along_x_v.at[there, part(h)],
                        along_x_v.at[there, part(h)],
                        x_send.at[d, h],
                        x_recv.at[there, h],
                        place(there, z, h),
                    ).wait_recv()
                window_v[3] += along_x_v[there]

        for h in range(CORES):
            halfway(1, h).wait_send()
        for e in far_first(nz):
            along(1, along_z_v.at[1, z], e).wait_send()
        inside(1, other).wait_send()
        for d in far_first(nx):

            @pl.when(x < lax.rem(x + d, nx))
            def _():
                for c in range(CORES):
                    across(d, c).wait_send()

    def pull():
        arrived("block", "dual_resource", "coef_production", "coef_setup")
        by_block_production = exact(dual_resource_v[...], coef_production_v[...], ((1,), (1,)))
        by_block_setup = exact(dual_resource_v[...], coef_setup_v[...], ((1,), (1,)))
        stacked = jnp.concatenate(
            [t.astype(F32) for t in halves(by_block_production, 3) + halves(by_block_setup, 3)], axis=0
        ).astype(BF16)
        wide = 4

        @pl.loop(0, chunks // wide)
        def _(i):
            for k in range(wide):
                j = i * wide + k
                ids = jnp.broadcast_to(block_v[pl.ds(j, 1), :], (blocks, LANES))
                hot = ids == lax.broadcasted_iota(jnp.int32, (blocks, LANES), 0)
                onehot_v[:, lanes(j)] = jnp.where(hot, 1.0, 0.0).astype(BF16)
            at = pl.ds(pl.multiple_of(i * wide * LANES, wide * LANES), wide * LANES)
            pulled = jnp.dot(stacked, onehot_v[:, at], preferred_element_type=F32)
            pull_production_v[:, at] = pulled[0:rows] + (
                pulled[rows : 2 * rows] + pulled[2 * rows : 3 * rows]
            )
            pull_setup_v[:, at] = pulled[3 * rows : 4 * rows] + (
                pulled[4 * rows : 5 * rows] + pulled[5 * rows : 6 * rows]
            )

    def used(bar_v, coef_v):
        deep = DEPTH * LANES

        def add_blocks(i, total):
            at = pl.ds(pl.multiple_of(i * deep, deep), deep)
            left = jnp.concatenate(halves(bar_v[:, at], 2), axis=0)
            return total + lax.dot_general(
                left, onehot_v[:, at], (((1,), (1,)), ((), ())), preferred_element_type=F32
            )

        by_block = lax.fori_loop(0, items // deep, add_blocks, jnp.zeros((2 * rows, blocks), F32))
        return exact(by_block[0:rows] + by_block[rows : 2 * rows], coef_v[...], ((1,), (0,)))

    def own_part():
        arrived(
            "cost_setup",
            "penalty",
            "dual_link",
            "setup",
            "fixing",
            "shortage",
            "production",
            "cost_production",
        )

        @pl.loop(0, chunks)
        def _(j):
            begin, stop, active = window(j)
            setup_price = row(cost_setup_v, j)
            late_price = row(penalty_v, j)
            for g in range(groups):
                on = active[g]
                dual_active = jnp.where(on, piece(dual_demand_v, g, j), 0.0)
                link_active = jnp.where(on, piece(dual_link_v, g, j), 0.0)
                primal_step = 1.0 / (2.0 + jnp.maximum(stop - period[g], 0.0))
                dual_step = 1.0 / (2.0 + jnp.maximum(period[g] - begin, 0.0))
                price = (
                    piece(cost_production_v, g, j)
                    - piece(local_v, g, j)
                    + link_active
                    + piece(pull_production_v, g, j)
                )
                put(local_v, g, j, piece(production_v, g, j) - primal_step * price)
                put(primal_step_v, g, j, primal_step)
                put(dual_step_v, g, j, dual_step)
                before = piece(setup_v, g, j)
                moved = jnp.clip(
                    before - setup_step * (setup_price - big_m * link_active + piece(pull_setup_v, g, j)),
                    0.0,
                    1.0,
                )
                state = piece(fixing_v, g, j)
                moved = jnp.where(state == 1, 0.0, jnp.where(state == 2, 1.0, moved))
                moved = jnp.where(on, moved, 0.0)
                put(setup_v, g, j, moved)
                setup_bar = jnp.where(on, 2.0 * moved - before, 0.0)
                put(setup_bar_v, g, j, setup_bar)
                put(link_v, g, j, link_active - link_step * big_m * setup_bar)
                before = piece(shortage_v, g, j)
                late = jnp.where(
                    on, jnp.maximum(before - short_step * (late_price - dual_active), 0.0), 0.0
                )
                put(shortage_v, g, j, late)
                put(dual_demand_v, g, j, dual_active - dual_step * (2.0 * late - before))

    def own_and_usage():
        own_part()
        usage_v[y] = used(setup_bar_v, coef_setup_v)

    suffix_scan(pull, own_and_usage)
    arrived("demand")

    def net_production(j):
        begin, stop, active = window(j)
        carry = row(window_v.at[2], j)
        total = jnp.zeros((GROUP, LANES), F32)
        for g in range(groups):
            on = active[g]
            before = piece(production_v, g, j)
            made = jnp.maximum(piece(local_v, g, j) + piece(primal_step_v, g, j) * carry, 0.0)
            made = jnp.where(on, made, 0.0)
            put(production_v, g, j, made)
            bar = jnp.where(on, 2.0 * made - before, 0.0)
            put(prod_bar_v, g, j, bar)
            total = total + (bar - jnp.where(on, piece(demand_v, g, j), 0.0))
        own_v[1, pl.ds(j, 1), :] = jnp.sum(total, axis=0, keepdims=True)

    def net_half(h):
        @pl.loop(0, half // UNROLL)
        def _(i):
            for k in range(UNROLL):
                net_production(h * half + i * UNROLL + k)

        halfway(1, h).start()

    net_half(core)
    suffix_other()
    net_half(1 - core)

    def beside(d):
        return remote(
            usage_v.at[y], usage_v.at[y], y_send.at[d], y_recv.at[y], place(x, z, core, lax.rem(y + d, ny))
        )

    def dual_part():
        usage_v[y] += used(prod_bar_v, coef_production_v)
        for d in range(1, ny):
            beside(d).start()

        @pl.loop(0, chunks)
        def _(j):
            begin, stop, active = window(j)
            flow = [
                piece(prod_bar_v, g, j) - jnp.where(active[g], piece(demand_v, g, j), 0.0)
                for g in range(groups)
            ]
            heads = prefix_rows(flow, sub)
            for g in range(groups):
                put(
                    dual_demand_v,
                    g,
                    j,
                    piece(dual_demand_v, g, j) - piece(dual_step_v, g, j) * heads[g],
                )
                link = jnp.maximum(piece(link_v, g, j) + link_step * piece(prod_bar_v, g, j), 0.0)
                put(dual_link_v, g, j, jnp.where(active[g], link, 0.0))

    def resource_part():
        for d in range(1, ny):
            beside(d).wait_send()
        for d in range(1, ny):
            there = lax.rem(y + d, ny)
            remote(
                usage_v.at[there], usage_v.at[there], y_send.at[d], y_recv.at[there], place(x, z, core, there)
            ).wait_recv()
        arrived("capacity")
        usage = usage_v[0]
        for k in range(1, ny):
            usage = usage + usage_v[k]
        scale = dual_resource_v.shape[1] / items_total
        dual_resource_v[...] = jnp.maximum(dual_resource_v[...] + scale * (usage - capacity_v[...]), 0.0)

    prefix_scan(dual_part, suffix_left)
    resource_part()


def finish(
    production_v,
    setup_v,
    shortage_v,
    dual_demand_v,
    dual_link_v,
    dual_resource_v,
    dual_step_v,
    window_v,
    production_o,
    setup_o,
    shortage_o,
    dual_demand_o,
    dual_link_o,
    dual_resource_o,
    result_v,
    out_sem,
):
    pairs = [
        (production_v, production_o),
        (setup_v, setup_o),
        (shortage_v, shortage_o),
        (dual_link_v, dual_link_o),
        (dual_resource_v, dual_resource_o),
    ]
    copies = [pltpu.make_async_copy(src, dst, out_sem.at[k]) for k, (src, dst) in enumerate(pairs)]
    for copy in copies:
        copy.start()
    rows, items = result_v.shape
    first = (lax.axis_index("tm") * rows).astype(F32)
    sub = lax.broadcasted_iota(jnp.int32, (GROUP, LANES), 0).astype(F32)

    step = items // PIECES
    for p in range(PIECES):

        @pl.loop(p * step // LANES, (p + 1) * step // LANES, step=2)
        def _(i):
            for j in (i, i + 1):
                at = pl.ds(pl.multiple_of(j * LANES, LANES), LANES)
                begin, stop, carry = [
                    jnp.broadcast_to(window_v[k, pl.ds(j, 1), :], (GROUP, LANES)) for k in (0, 1, 3)
                ]
                for g in range(rows // GROUP):
                    t = sub + (first + float(g * GROUP))
                    band = slice(g * GROUP, (g + 1) * GROUP)
                    dual = jnp.maximum(dual_demand_v[band, at] - dual_step_v[band, at] * carry, 0.0)
                    result_v[band, at] = jnp.where((t >= begin) & (t <= stop), dual, 0.0)

        at = pl.ds(p * step, step)
        copies.append(
            pltpu.make_async_copy(result_v.at[:, at], dual_demand_o.at[:, at], out_sem.at[len(pairs) + p])
        )
        copies[-1].start()

    for copy in copies:
        copy.wait()


def shards(ranks, items_total, *args):
    (
        production,
        setup,
        shortage,
        dual_demand,
        dual_link,
        dual_resource,
        cost_production,
        cost_setup,
        penalty,
        demand,
        capacity,
        coef_production,
        coef_setup,
        horizon_start,
        horizon_end,
        fixing,
        block_id,
    ) = args
    nx, nz, ny = ranks
    rows, items = production.shape
    resources = dual_resource.shape[1]
    blocks = coef_production.shape[0]
    chunks = items // LANES
    per_item = (chunks, LANES)
    big, vector, small = (rows, items), (chunks, LANES), (rows, resources)

    def vmem(shape, dtype=F32):
        return pltpu.VMEM(shape, dtype)

    dma = pltpu.SemaphoreType.DMA
    anywhere = pl.BlockSpec(memory_space=pl.ANY)
    scratch = (
        [vmem(big)] * 2
        + [vmem(big, jnp.int32)]
        + [vmem(small)]
        + [vmem((blocks, resources))] * 2
        + [vmem(vector)] * 2
        + [vmem(vector, jnp.int32)] * 3
        + [vmem((blocks, items), BF16)]
        + [vmem(big)] * 7
        + [
            vmem((2,) + vector),
            vmem((2,) + vector),
            vmem((2, nz, chunks // 2, LANES)),
            vmem((nx,) + vector),
            vmem((2,) + vector),
            vmem((nx, CORES, chunks // 2, LANES)),
            vmem((2, chunks // 2, LANES)),
            vmem((ny,) + small),
        ]
        + [
            dma((17,)),
            dma((2, CORES)),
            dma((2, CORES)),
            dma((2, nz)),
            dma((2, nz)),
            dma((nx, CORES)),
            dma((nx, CORES)),
            dma((2,)),
            dma((2,)),
            dma((nx, CORES)),
            dma((nx, CORES)),
            pltpu.SemaphoreType.REGULAR,
            dma((ny,)),
            dma((ny,)),
        ]
    )
    operands = [
        production,
        setup,
        shortage,
        dual_demand,
        dual_link,
        dual_resource,
        cost_production,
        cost_setup.reshape(per_item),
        penalty.reshape(per_item),
        demand,
        capacity,
        coef_production,
        coef_setup,
        horizon_start.reshape(per_item),
        horizon_end.reshape(per_item),
        fixing,
        block_id.reshape(per_item),
    ]
    operands = [pltpu.with_memory_space_constraint(a, pltpu.HBM) for a in operands]
    held = pl.BlockSpec(memory_space=pltpu.VMEM)
    between = [big] * 5 + [small, big, (4,) + vector]
    parts = pl.pallas_call(
        functools.partial(kernel, ranks, items_total),
        out_shape=[pltpu.VMEM(shape, F32) for shape in between],
        in_specs=[anywhere] * 17,
        out_specs=[held] * len(between),
        scratch_shapes=scratch,
        compiler_params=pltpu.CompilerParams(
            collective_id=0, has_side_effects=True, vmem_limit_bytes=40 * 1024 * 1024
        ),
        name="lot_step",
    )(*operands)
    results = pl.pallas_call(
        finish,
        out_shape=[jax.ShapeDtypeStruct(big, F32)] * 5 + [jax.ShapeDtypeStruct(small, F32)],
        in_specs=[held] * len(between),
        out_specs=[anywhere] * 6,
        scratch_shapes=[vmem(big), dma((5 + PIECES,))],
        compiler_params=pltpu.CompilerParams(vmem_limit_bytes=8 * 1024 * 1024),
        name="finish",
    )(*parts)
    return tuple(results)


def solution(mesh):
    across, ny = mesh.shape["tm"], mesh.shape["items"]
    nz = 8
    nx = across // (nz * CORES)
    placed = (
        P("tm", "items"),
        P("tm", "items"),
        P("tm", "items"),
        P("tm", "items"),
        P("tm", "items"),
        P("tm", None),
        P("tm", "items"),
        P("items"),
        P("items"),
        P("tm", "items"),
        P("tm", None),
        P(),
        P(),
        P("items"),
        P("items"),
        P("tm", "items"),
        P("items"),
    )

    def step(*args):
        return jax.shard_map(
            functools.partial(shards, (nx, nz, ny), args[0].shape[1]),
            mesh=mesh,
            in_specs=placed,
            out_specs=(P("tm", "items"),) * 5 + (P("tm", None),),
            check_vma=False,
        )(*args)

    return step
```

```python
import functools

import jax
import jax.numpy as jnp
from jax import lax
from jax.experimental import pallas as pl
from jax.experimental.pallas import tpu as pltpu
from jax.sharding import PartitionSpec as P

MESH = pl.DeviceIdType.MESH
F32 = jnp.float32
BF16 = jnp.bfloat16

big_m = 4.0
setup_step = 0.5
short_step = 0.5
link_step = 0.25

LANES = 128
GROUP = 8
CORES = 2
DEPTH = 16
UNROLL = 16
RELAY = 2
PIECES = 2


def suffix_rows(groups, sub):
    tail = jnp.zeros((GROUP, LANES), F32)
    out = [None] * len(groups)
    for g in reversed(range(len(groups))):
        part = groups[g]
        for shift in (1, 2, 4):
            moved = pltpu.roll(part, GROUP - shift, 0)
            part = part + jnp.where(sub < GROUP - shift, moved, 0.0)
        out[g] = part + tail
        tail = jnp.broadcast_to(out[g][0:1, :], (GROUP, LANES))
    return out, tail


def prefix_rows(groups, sub):
    head = jnp.zeros((GROUP, LANES), F32)
    out = [None] * len(groups)
    for g in range(len(groups)):
        part = groups[g]
        for shift in (1, 2, 4):
            moved = pltpu.roll(part, shift, 0)
            part = part + jnp.where(sub >= shift, moved, 0.0)
        out[g] = part + head
        head = jnp.broadcast_to(out[g][GROUP - 1 :, :], (GROUP, LANES))
    return out


def halves(value, count):
    terms = []
    for k in range(count):
        term = value.astype(BF16)
        terms.append(term)
        if k + 1 < count:
            value = value - term.astype(F32)
    return terms


def far_first(count):
    return sorted(range(1, count), key=lambda d: -min(d, count - d))


def exact(left, right, contract):
    return lax.dot_general(
        left, right, (contract, ((), ())), precision=lax.Precision.HIGHEST, preferred_element_type=F32
    )


def kernel(
    ranks,
    items_total,
    production_h,
    setup_h,
    shortage_h,
    dual_demand_h,
    dual_link_h,
    dual_resource_h,
    cost_production_h,
    cost_setup_h,
    penalty_h,
    demand_h,
    capacity_h,
    coef_production_h,
    coef_setup_h,
    start_h,
    end_h,
    fixing_h,
    block_h,
    production_v,
    setup_v,
    shortage_v,
    dual_demand_v,
    dual_link_v,
    dual_resource_v,
    dual_step_v,
    window_v,
    cost_production_v,
    demand_v,
    fixing_v,
    capacity_v,
    coef_production_v,
    coef_setup_v,
    cost_setup_v,
    penalty_v,
    start_v,
    end_v,
    block_v,
    onehot_v,
    pull_production_v,
    pull_setup_v,
    local_v,
    primal_step_v,
    given_v,
    fixed_v,
    setup_bar_v,
    prod_bar_v,
    link_v,
    own_v,
    sibling_v,
    along_z_v,
    along_x_v,
    inside_v,
    raw_x_v,
    column_v,
    usage_v,
    in_sem,
    core_send,
    core_recv,
    z_send,
    z_recv,
    x_send,
    x_recv,
    inside_send,
    inside_recv,
    raw_send,
    raw_recv,
    ready,
    y_send,
    y_recv,
):
    nx, nz, ny = ranks
    rows, items = production_v.shape
    groups = rows // GROUP
    chunks = items // LANES
    half = chunks // 2
    blocks = coef_production_v.shape[0]
    tm = lax.axis_index("tm")
    y = lax.axis_index("items")
    core = lax.rem(tm, CORES)
    z = lax.rem(tm // CORES, nz)
    x = tm // (CORES * nz)

    def place(px, pz, pc, py=None):
        return ((px * nz + pz) * CORES + pc, y if py is None else py)

    barrier = pltpu.get_barrier_semaphore()
    greeted = 0
    for d in [d for d in far_first(nz) if min(d, nz - d) <= RELAY]:
        pl.semaphore_signal(
            barrier, inc=1, device_id=place(x, lax.rem(z + d, nz), core), device_id_type=MESH
        )
        greeted += 1
    for d in far_first(nx):
        for c in range(CORES):
            pl.semaphore_signal(
                barrier, inc=1, device_id=place(lax.rem(x + d, nx), z, c), device_id_type=MESH
            )
            greeted += 1
    for d in range(1, ny):
        pl.semaphore_signal(
            barrier, inc=1, device_id=place(x, z, core, lax.rem(y + d, ny)), device_id_type=MESH
        )
        greeted += 1
    pl.semaphore_signal(barrier, inc=1, device_id=place(x, z, 1 - core), device_id_type=MESH)
    greeted += 1

    loads = {
        "start": (start_h, start_v),
        "end": (end_h, end_v),
        "dual_demand": (dual_demand_h, dual_demand_v),
        "block": (block_h, block_v),
        "dual_resource": (dual_resource_h, dual_resource_v),
        "coef_production": (coef_production_h, coef_production_v),
        "coef_setup": (coef_setup_h, coef_setup_v),
        "cost_setup": (cost_setup_h, cost_setup_v),
        "penalty": (penalty_h, penalty_v),
        "dual_link": (dual_link_h, dual_link_v),
        "setup": (setup_h, setup_v),
        "fixing": (fixing_h, fixing_v),
        "shortage": (shortage_h, shortage_v),
        "production": (production_h, given_v),
        "cost_production": (cost_production_h, cost_production_v),
        "demand": (demand_h, demand_v),
        "capacity": (capacity_h, capacity_v),
    }
    load = {
        name: pltpu.make_async_copy(src, dst, in_sem.at[k])
        for k, (name, (src, dst)) in enumerate(loads.items())
    }
    for copy in load.values():
        copy.start()

    def arrived(*names):
        for name in names:
            load[name].wait()

    sub = lax.broadcasted_iota(jnp.int32, (GROUP, LANES), 0)
    first = (tm * rows).astype(F32)
    period = [sub.astype(F32) + (first + float(g * GROUP)) for g in range(groups)]

    def lanes(j):
        return pl.ds(pl.multiple_of(j * LANES, LANES), LANES)

    def piece(ref, g, j):
        return ref[g * GROUP : (g + 1) * GROUP, lanes(j)]

    def put(ref, g, j, value):
        ref[g * GROUP : (g + 1) * GROUP, lanes(j)] = value

    def row(ref, j):
        return jnp.broadcast_to(ref[pl.ds(j, 1), :], (GROUP, LANES))

    def window(j):
        begin, stop = row(window_v.at[0], j), row(window_v.at[1], j)
        return begin, stop, [(t >= begin) & (t <= stop) for t in period]

    arrived("start", "end")
    window_v[0] = start_v[...].astype(F32)
    window_v[1] = end_v[...].astype(F32)

    arrived("dual_demand")

    @pl.loop(0, chunks)
    def _(j):
        begin, stop, active = window(j)
        parts = [jnp.where(active[g], piece(dual_demand_v, g, j), 0.0) for g in range(groups)]
        tails, total = suffix_rows(parts, sub)
        for g in range(groups):
            put(local_v, g, j, tails[g])
        own_v[0, pl.ds(j, 1), :] = total[0:1, :]

    pl.semaphore_wait(barrier, greeted)

    def remote(src, dst, send, recv, where):
        return pltpu.make_async_remote_copy(
            src_ref=src, dst_ref=dst, send_sem=send, recv_sem=recv, device_id=where, device_id_type=MESH
        )

    def part(h):
        return pl.ds(pl.multiple_of(h * half, half), half)

    sibling = place(x, z, 1 - core)
    mine, other = part(core), part(1 - core)

    def halfway(s, h):
        return remote(
            own_v.at[s, part(h)], sibling_v.at[s, part(h)], core_send.at[s, h], core_recv.at[s, h], sibling
        )

    def along(s, src, e):
        return remote(
            src, along_z_v.at[s, z], z_send.at[s, e], z_recv.at[s, z], place(x, lax.rem(z + e, nz), core)
        )

    def from_along(s, e):
        there = lax.rem(z + e, nz)
        remote(
            along_z_v.at[s, there],
            along_z_v.at[s, there],
            z_send.at[s, e],
            z_recv.at[s, there],
            place(x, there, core),
        ).wait_recv()
        return along_z_v[s, there]

    def raw(d, c):
        return remote(
            own_v.at[0, part(c)],
            raw_x_v.at[x, core],
            raw_send.at[d, c],
            raw_recv.at[x, core],
            place(lax.rem(x + d, nx), z, c),
        )

    def across(d, c):
        return remote(
            along_x_v.at[x, other],
            along_x_v.at[x, other],
            x_send.at[d, c],
            x_recv.at[x, 1 - core],
            place(lax.rem(x + d, nx), z, c),
        )

    def inside(s, where):
        return remote(
            inside_v.at[s, where], inside_v.at[s, where], inside_send.at[s], inside_recv.at[s], sibling
        )

    def column(e):
        there = lax.rem(z + e, nz)
        return along(0, column_v.at[jnp.where(z > there, 1, 0)], e)

    later_core = core == 0

    def suffix_scan(during_x, during_z):
        for d in far_first(nx):

            @pl.when(x > lax.rem(x + d, nx))
            def _():
                for c in range(CORES):
                    raw(d, c).start()

        halfway(0, 1 - core).start()
        halfway(0, core).start()
        for e in (RELAY, nz - RELAY):
            pl.semaphore_signal(
                ready, inc=1, device_id=place(x, lax.rem(z + e, nz), core), device_id_type=MESH
            )
        during_x()
        halfway(0, core).wait_recv()
        column_v[0] = jnp.zeros((half, LANES), F32)
        for d in reversed(far_first(nx)):
            there = lax.rem(x + d, nx)

            @pl.when(there > x)
            def _():
                for c in range(CORES):
                    remote(
                        raw_x_v.at[there, c],
                        raw_x_v.at[there, c],
                        raw_send.at[d, c],
                        raw_recv.at[there, c],
                        place(there, z, c),
                    ).wait_recv()
                column_v[0] += raw_x_v[there, 0] + raw_x_v[there, 1]

        column_v[1] = column_v[0] + (own_v[0, mine, :] + sibling_v[0, mine, :])
        pl.semaphore_wait(ready, 2)
        for e in far_first(nz):
            column(e).start()
        during_z()
        total = column_v[0]
        for e in reversed(far_first(nz)):
            total = total + from_along(0, e)
        inside_v[0, mine, :] = total
        inside(0, mine).start()
        window_v[2, mine, :] = total + jnp.where(later_core, sibling_v[0, mine, :], 0.0)

    def suffix_other():
        halfway(0, 1 - core).wait_recv()
        inside(0, other).wait_recv()
        window_v[2, other, :] = inside_v[0, other, :] + jnp.where(
            later_core, sibling_v[0, other, :], 0.0
        )

    def suffix_left():
        for d in far_first(nx):

            @pl.when(x > lax.rem(x + d, nx))
            def _():
                for c in range(CORES):
                    raw(d, c).wait_send()

        for h in range(CORES):
            halfway(0, h).wait_send()
        for e in far_first(nz):
            column(e).wait_send()
        inside(0, mine).wait_send()

    def prefix_scan(during_z, during_x):
        halfway(1, 1 - core).wait_recv()
        along_z_v[1, z] = own_v[1, other, :] + sibling_v[1, other, :]
        for e in far_first(nz):
            along(1, along_z_v.at[1, z], e).start()
        during_z()
        whole = along_z_v[1, z]
        partial = jnp.zeros_like(whole)
        for e in reversed(far_first(nz)):
            term = from_along(1, e)
            whole = whole + term
            partial = partial + jnp.where(lax.rem(z + e, nz) < z, term, 0.0)
        inside_v[1, other, :] = partial
        inside(1, other).start()
        along_x_v[x, other, :] = whole
        for d in far_first(nx):

            @pl.when(x < lax.rem(x + d, nx))
            def _():
                for c in range(CORES):
                    across(d, c).start()

        during_x()
        halfway(1, core).wait_recv()
        inside(1, mine).wait_recv()
        for h in range(CORES):
            halfway(1, h).wait_send()
        for e in far_first(nz):
            along(1, along_z_v.at[1, z], e).wait_send()
        window_v[3] = inside_v[1] + jnp.where(later_core, 0.0, sibling_v[1])
        for d in reversed(far_first(nx)):
            there = lax.rem(x + d, nx)

            @pl.when(there < x)
            def _():
                for h in range(CORES):
                    remote(
                        along_x_v.at[there, part(h)],
                        along_x_v.at[there, part(h)],
                        x_send.at[d, h],
                        x_recv.at[there, h],
                        place(there, z, h),
                    ).wait_recv()
                window_v[3] += along_x_v[there]

        inside(1, other).wait_send()
        for d in far_first(nx):

            @pl.when(x < lax.rem(x + d, nx))
            def _():
                for c in range(CORES):
                    across(d, c).wait_send()

    wide = 4

    def pull():
        arrived("block", "dual_resource", "coef_production", "coef_setup")
        by_block_production = exact(dual_resource_v[...], coef_production_v[...], ((1,), (1,)))
        by_block_setup = exact(dual_resource_v[...], coef_setup_v[...], ((1,), (1,)))
        stacked = jnp.concatenate(
            [t.astype(F32) for t in halves(by_block_production, 3) + halves(by_block_setup, 3)], axis=0
        ).astype(BF16)

        @pl.loop(0, chunks // wide)
        def _(i):
            for k in range(wide):
                j = i * wide + k
                ids = jnp.broadcast_to(block_v[pl.ds(j, 1), :], (blocks, LANES))
                hot = ids == lax.broadcasted_iota(jnp.int32, (blocks, LANES), 0)
                onehot_v[:, lanes(j)] = jnp.where(hot, 1.0, 0.0).astype(BF16)
            at = pl.ds(pl.multiple_of(i * wide * LANES, wide * LANES), wide * LANES)
            pulled = jnp.dot(stacked, onehot_v[:, at], preferred_element_type=F32)
            pull_production_v[:, at] = pulled[0:rows] + (
                pulled[rows : 2 * rows] + pulled[2 * rows : 3 * rows]
            )
            pull_setup_v[:, at] = pulled[3 * rows : 4 * rows] + (
                pulled[4 * rows : 5 * rows] + pulled[5 * rows : 6 * rows]
            )

    def used(bar_v, coef_v):
        deep = DEPTH * LANES

        def add_blocks(i, total):
            at = pl.ds(pl.multiple_of(i * deep, deep), deep)
            left = jnp.concatenate(halves(bar_v[:, at], 2), axis=0)
            return total + lax.dot_general(
                left, onehot_v[:, at], (((1,), (1,)), ((), ())), preferred_element_type=F32
            )

        by_block = lax.fori_loop(0, items // deep, add_blocks, jnp.zeros((2 * rows, blocks), F32))
        return exact(by_block[0:rows] + by_block[rows : 2 * rows], coef_v[...], ((1,), (0,)))

    def own_part():
        arrived(
            "cost_setup",
            "penalty",
            "dual_link",
            "setup",
            "fixing",
            "shortage",
            "production",
            "cost_production",
            "demand",
        )

        @pl.loop(0, chunks)
        def _(j):
            begin, stop, active = window(j)
            setup_price = row(cost_setup_v, j)
            late_price = row(penalty_v, j)
            fixed = jnp.zeros((GROUP, LANES), F32)
            for g in range(groups):
                on = active[g]
                dual_active = jnp.where(on, piece(dual_demand_v, g, j), 0.0)
                link_active = jnp.where(on, piece(dual_link_v, g, j), 0.0)
                primal_step = 1.0 / (2.0 + jnp.maximum(stop - period[g], 0.0))
                dual_step = 1.0 / (2.0 + jnp.maximum(period[g] - begin, 0.0))
                price = (
                    piece(cost_production_v, g, j)
                    - piece(local_v, g, j)
                    + link_active
                    + piece(pull_production_v, g, j)
                )
                before = piece(given_v, g, j)
                put(local_v, g, j, jnp.where(on, before - primal_step * price, 0.0))
                put(primal_step_v, g, j, jnp.where(on, primal_step, 0.0))
                fixed = fixed + jnp.where(on, before + piece(demand_v, g, j), 0.0)
                put(dual_step_v, g, j, dual_step)
                before = piece(setup_v, g, j)
                moved = jnp.clip(
                    before - setup_step * (setup_price - big_m * link_active + piece(pull_setup_v, g, j)),
                    0.0,
                    1.0,
                )
                state = piece(fixing_v, g, j)
                moved = jnp.where(state == 1, 0.0, jnp.where(state == 2, 1.0, moved))
                moved = jnp.where(on, moved, 0.0)
                put(setup_v, g, j, moved)
                setup_bar = jnp.where(on, 2.0 * moved - before, 0.0)
                put(setup_bar_v, g, j, setup_bar)
                put(link_v, g, j, link_active - link_step * big_m * setup_bar)
                before = piece(shortage_v, g, j)
                late = jnp.where(
                    on, jnp.maximum(before - short_step * (late_price - dual_active), 0.0), 0.0
                )
                put(shortage_v, g, j, late)
                put(dual_demand_v, g, j, dual_active - dual_step * (2.0 * late - before))
            fixed_v[pl.ds(j, 1), :] = jnp.sum(fixed, axis=0, keepdims=True)

    def own_and_usage():
        own_part()
        usage_v[y] = used(setup_bar_v, coef_setup_v)

    suffix_scan(pull, own_and_usage)
    def net_production(j):
        carry = row(window_v.at[2], j)
        total = jnp.zeros((GROUP, LANES), F32)
        for g in range(groups):
            made = jnp.maximum(piece(local_v, g, j) + piece(primal_step_v, g, j) * carry, 0.0)
            put(production_v, g, j, made)
            total = total + made
        own_v[1, pl.ds(j, 1), :] = (
            2.0 * jnp.sum(total, axis=0, keepdims=True) - fixed_v[pl.ds(j, 1), :]
        )

    def net_half(h):
        @pl.loop(0, half // UNROLL)
        def _(i):
            for k in range(UNROLL):
                net_production(h * half + i * UNROLL + k)

        halfway(1, h).start()

    net_half(core)
    suffix_other()
    net_half(1 - core)

    def beside(d):
        return remote(
            usage_v.at[y], usage_v.at[y], y_send.at[d], y_recv.at[y], place(x, z, core, lax.rem(y + d, ny))
        )

    def dual_part():
        @pl.loop(0, chunks // wide)
        def _(i):
            for k in range(wide):
                j = i * wide + k
                begin, stop, active = window(j)
                for g in range(groups):
                    bar = 2.0 * piece(production_v, g, j) - piece(given_v, g, j)
                    put(prod_bar_v, g, j, jnp.where(active[g], bar, 0.0))

        usage_v[y] += used(prod_bar_v, coef_production_v)
        for d in range(1, ny):
            beside(d).start()

        @pl.loop(0, chunks)
        def _(j):
            begin, stop, active = window(j)
            flow = [
                piece(prod_bar_v, g, j) - jnp.where(active[g], piece(demand_v, g, j), 0.0)
                for g in range(groups)
            ]
            heads = prefix_rows(flow, sub)
            for g in range(groups):
                put(
                    dual_demand_v,
                    g,
                    j,
                    piece(dual_demand_v, g, j) - piece(dual_step_v, g, j) * heads[g],
                )
                link = jnp.maximum(piece(link_v, g, j) + link_step * piece(prod_bar_v, g, j), 0.0)
                put(dual_link_v, g, j, jnp.where(active[g], link, 0.0))

    def resource_part():
        for d in range(1, ny):
            beside(d).wait_send()
        for d in range(1, ny):
            there = lax.rem(y + d, ny)
            remote(
                usage_v.at[there], usage_v.at[there], y_send.at[d], y_recv.at[there], place(x, z, core, there)
            ).wait_recv()
        arrived("capacity")
        usage = usage_v[0]
        for k in range(1, ny):
            usage = usage + usage_v[k]
        scale = dual_resource_v.shape[1] / items_total
        dual_resource_v[...] = jnp.maximum(dual_resource_v[...] + scale * (usage - capacity_v[...]), 0.0)

    def dual_and_left():
        dual_part()
        suffix_left()

    prefix_scan(dual_and_left, resource_part)


def finish(
    production_v,
    setup_v,
    shortage_v,
    dual_demand_v,
    dual_link_v,
    dual_resource_v,
    dual_step_v,
    window_v,
    production_o,
    setup_o,
    shortage_o,
    dual_demand_o,
    dual_link_o,
    dual_resource_o,
    result_v,
    out_sem,
):
    pairs = [
        (production_v, production_o),
        (setup_v, setup_o),
        (shortage_v, shortage_o),
        (dual_link_v, dual_link_o),
        (dual_resource_v, dual_resource_o),
    ]
    copies = [pltpu.make_async_copy(src, dst, out_sem.at[k]) for k, (src, dst) in enumerate(pairs)]
    for copy in copies:
        copy.start()
    rows, items = result_v.shape
    first = (lax.axis_index("tm") * rows).astype(F32)
    sub = lax.broadcasted_iota(jnp.int32, (GROUP, LANES), 0).astype(F32)

    step = items // PIECES
    for p in range(PIECES):

        @pl.loop(p * step // LANES, (p + 1) * step // LANES, step=2)
        def _(i):
            for j in (i, i + 1):
                at = pl.ds(pl.multiple_of(j * LANES, LANES), LANES)
                begin, stop, carry = [
                    jnp.broadcast_to(window_v[k, pl.ds(j, 1), :], (GROUP, LANES)) for k in (0, 1, 3)
                ]
                for g in range(rows // GROUP):
                    t = sub + (first + float(g * GROUP))
                    band = slice(g * GROUP, (g + 1) * GROUP)
                    dual = jnp.maximum(dual_demand_v[band, at] - dual_step_v[band, at] * carry, 0.0)
                    result_v[band, at] = jnp.where((t >= begin) & (t <= stop), dual, 0.0)

        at = pl.ds(p * step, step)
        copies.append(
            pltpu.make_async_copy(result_v.at[:, at], dual_demand_o.at[:, at], out_sem.at[len(pairs) + p])
        )
        copies[-1].start()

    for copy in copies:
        copy.wait()


def shards(ranks, items_total, *args):
    (
        production,
        setup,
        shortage,
        dual_demand,
        dual_link,
        dual_resource,
        cost_production,
        cost_setup,
        penalty,
        demand,
        capacity,
        coef_production,
        coef_setup,
        horizon_start,
        horizon_end,
        fixing,
        block_id,
    ) = args
    nx, nz, ny = ranks
    rows, items = production.shape
    resources = dual_resource.shape[1]
    blocks = coef_production.shape[0]
    chunks = items // LANES
    per_item = (chunks, LANES)
    big, vector, small = (rows, items), (chunks, LANES), (rows, resources)

    def vmem(shape, dtype=F32):
        return pltpu.VMEM(shape, dtype)

    dma = pltpu.SemaphoreType.DMA
    anywhere = pl.BlockSpec(memory_space=pl.ANY)
    scratch = (
        [vmem(big)] * 2
        + [vmem(big, jnp.int32)]
        + [vmem(small)]
        + [vmem((blocks, resources))] * 2
        + [vmem(vector)] * 2
        + [vmem(vector, jnp.int32)] * 3
        + [vmem((blocks, items), BF16)]
        + [vmem(big)] * 5
        + [vmem(vector)]
        + [vmem(big)] * 3
        + [
            vmem((2,) + vector),
            vmem((2,) + vector),
            vmem((2, nz, chunks // 2, LANES)),
            vmem((nx,) + vector),
            vmem((2,) + vector),
            vmem((nx, CORES, chunks // 2, LANES)),
            vmem((2, chunks // 2, LANES)),
            vmem((ny,) + small),
        ]
        + [
            dma((17,)),
            dma((2, CORES)),
            dma((2, CORES)),
            dma((2, nz)),
            dma((2, nz)),
            dma((nx, CORES)),
            dma((nx, CORES)),
            dma((2,)),
            dma((2,)),
            dma((nx, CORES)),
            dma((nx, CORES)),
            pltpu.SemaphoreType.REGULAR,
            dma((ny,)),
            dma((ny,)),
        ]
    )
    operands = [
        production,
        setup,
        shortage,
        dual_demand,
        dual_link,
        dual_resource,
        cost_production,
        cost_setup.reshape(per_item),
        penalty.reshape(per_item),
        demand,
        capacity,
        coef_production,
        coef_setup,
        horizon_start.reshape(per_item),
        horizon_end.reshape(per_item),
        fixing,
        block_id.reshape(per_item),
    ]
    operands = [pltpu.with_memory_space_constraint(a, pltpu.HBM) for a in operands]
    held = pl.BlockSpec(memory_space=pltpu.VMEM)
    between = [big] * 5 + [small, big, (4,) + vector]
    parts = pl.pallas_call(
        functools.partial(kernel, ranks, items_total),
        out_shape=[pltpu.VMEM(shape, F32) for shape in between],
        in_specs=[anywhere] * 17,
        out_specs=[held] * len(between),
        scratch_shapes=scratch,
        compiler_params=pltpu.CompilerParams(
            collective_id=0, has_side_effects=True, vmem_limit_bytes=40 * 1024 * 1024
        ),
        name="lot_step",
    )(*operands)
    results = pl.pallas_call(
        finish,
        out_shape=[jax.ShapeDtypeStruct(big, F32)] * 5 + [jax.ShapeDtypeStruct(small, F32)],
        in_specs=[held] * len(between),
        out_specs=[anywhere] * 6,
        scratch_shapes=[vmem(big), dma((5 + PIECES,))],
        compiler_params=pltpu.CompilerParams(vmem_limit_bytes=8 * 1024 * 1024),
        name="finish",
    )(*parts)
    return tuple(results)


def solution(mesh):
    across, ny = mesh.shape["tm"], mesh.shape["items"]
    nz = 8
    nx = across // (nz * CORES)
    placed = (
        P("tm", "items"),
        P("tm", "items"),
        P("tm", "items"),
        P("tm", "items"),
        P("tm", "items"),
        P("tm", None),
        P("tm", "items"),
        P("items"),
        P("items"),
        P("tm", "items"),
        P("tm", None),
        P(),
        P(),
        P("items"),
        P("items"),
        P("tm", "items"),
        P("items"),
    )

    def step(*args):
        return jax.shard_map(
            functools.partial(shards, (nx, nz, ny), args[0].shape[1]),
            mesh=mesh,
            in_specs=placed,
            out_specs=(P("tm", "items"),) * 5 + (P("tm", None),),
            check_vma=False,
        )(*args)

    return step
```

```python
import functools

import jax
import jax.numpy as jnp
from jax import lax
from jax.experimental import pallas as pl
from jax.experimental.pallas import tpu as pltpu
from jax.sharding import PartitionSpec as P

MESH = pl.DeviceIdType.MESH
F32 = jnp.float32
BF16 = jnp.bfloat16

big_m = 4.0
setup_step = 0.5
short_step = 0.5
link_step = 0.25

LANES = 128
GROUP = 8
CORES = 2
DEPTH = 16
UNROLL = 16
RELAY = 2
PIECES = 2


def suffix_rows(groups, sub):
    tail = jnp.zeros((GROUP, LANES), F32)
    out = [None] * len(groups)
    for g in reversed(range(len(groups))):
        part = groups[g]
        for shift in (1, 2, 4):
            moved = pltpu.roll(part, GROUP - shift, 0)
            part = part + jnp.where(sub < GROUP - shift, moved, 0.0)
        out[g] = part + tail
        tail = jnp.broadcast_to(out[g][0:1, :], (GROUP, LANES))
    return out, tail


def prefix_rows(groups, sub):
    head = jnp.zeros((GROUP, LANES), F32)
    out = [None] * len(groups)
    for g in range(len(groups)):
        part = groups[g]
        for shift in (1, 2, 4):
            moved = pltpu.roll(part, shift, 0)
            part = part + jnp.where(sub >= shift, moved, 0.0)
        out[g] = part + head
        head = jnp.broadcast_to(out[g][GROUP - 1 :, :], (GROUP, LANES))
    return out


def halves(value, count):
    terms = []
    for k in range(count):
        term = value.astype(BF16)
        terms.append(term)
        if k + 1 < count:
            value = value - term.astype(F32)
    return terms


def far_first(count):
    return sorted(range(1, count), key=lambda d: -min(d, count - d))


def exact(left, right, contract):
    return lax.dot_general(
        left, right, (contract, ((), ())), precision=lax.Precision.HIGHEST, preferred_element_type=F32
    )


def kernel(
    ranks,
    items_total,
    production_h,
    setup_h,
    shortage_h,
    dual_demand_h,
    dual_link_h,
    dual_resource_h,
    cost_production_h,
    cost_setup_h,
    penalty_h,
    demand_h,
    capacity_h,
    coef_production_h,
    coef_setup_h,
    start_h,
    end_h,
    fixing_h,
    block_h,
    production_v,
    setup_v,
    shortage_v,
    dual_demand_v,
    dual_link_v,
    dual_resource_v,
    dual_step_v,
    window_v,
    cost_production_v,
    demand_v,
    fixing_v,
    capacity_v,
    coef_production_v,
    coef_setup_v,
    cost_setup_v,
    penalty_v,
    start_v,
    end_v,
    block_v,
    onehot_v,
    pull_production_v,
    pull_setup_v,
    local_v,
    primal_step_v,
    given_v,
    fixed_v,
    setup_bar_v,
    prod_bar_v,
    link_v,
    own_v,
    sibling_v,
    along_z_v,
    along_x_v,
    inside_v,
    raw_x_v,
    column_v,
    usage_v,
    in_sem,
    core_send,
    core_recv,
    z_send,
    z_recv,
    x_send,
    x_recv,
    inside_send,
    inside_recv,
    raw_send,
    raw_recv,
    ready,
    y_send,
    y_recv,
):
    nx, nz, ny = ranks
    rows, items = production_v.shape
    groups = rows // GROUP
    chunks = items // LANES
    half = chunks // 2
    blocks = coef_production_v.shape[0]
    tm = lax.axis_index("tm")
    y = lax.axis_index("items")
    core = lax.rem(tm, CORES)
    z = lax.rem(tm // CORES, nz)
    x = tm // (CORES * nz)

    def place(px, pz, pc, py=None):
        return ((px * nz + pz) * CORES + pc, y if py is None else py)

    barrier = pltpu.get_barrier_semaphore()
    greetings = [(min(d, nz - d), place(x, lax.rem(z + d, nz), core)) for d in range(1, nz)]
    greetings = [(far, where) for far, where in greetings if far <= RELAY]
    for d in range(1, nx):
        for c in range(CORES):
            greetings.append((min(d, nx - d), place(lax.rem(x + d, nx), z, c)))
    for d in range(1, ny):
        greetings.append((min(d, ny - d), place(x, z, core, lax.rem(y + d, ny))))
    greetings.append((0, place(x, z, 1 - core)))
    for _, where in sorted(greetings, key=lambda item: -item[0]):
        pl.semaphore_signal(barrier, inc=1, device_id=where, device_id_type=MESH)
    greeted = len(greetings)

    loads = {
        "start": (start_h, start_v),
        "end": (end_h, end_v),
        "dual_demand": (dual_demand_h, dual_demand_v),
        "block": (block_h, block_v),
        "dual_resource": (dual_resource_h, dual_resource_v),
        "coef_production": (coef_production_h, coef_production_v),
        "coef_setup": (coef_setup_h, coef_setup_v),
        "cost_setup": (cost_setup_h, cost_setup_v),
        "penalty": (penalty_h, penalty_v),
        "dual_link": (dual_link_h, dual_link_v),
        "setup": (setup_h, setup_v),
        "fixing": (fixing_h, fixing_v),
        "shortage": (shortage_h, shortage_v),
        "production": (production_h, given_v),
        "cost_production": (cost_production_h, cost_production_v),
        "demand": (demand_h, demand_v),
        "capacity": (capacity_h, capacity_v),
    }
    load = {
        name: pltpu.make_async_copy(src, dst, in_sem.at[k])
        for k, (name, (src, dst)) in enumerate(loads.items())
    }
    for copy in load.values():
        copy.start()

    def arrived(*names):
        for name in names:
            load[name].wait()

    sub = lax.broadcasted_iota(jnp.int32, (GROUP, LANES), 0)
    first = (tm * rows).astype(F32)
    period = [sub.astype(F32) + (first + float(g * GROUP)) for g in range(groups)]

    def lanes(j):
        return pl.ds(pl.multiple_of(j * LANES, LANES), LANES)

    def piece(ref, g, j):
        return ref[g * GROUP : (g + 1) * GROUP, lanes(j)]

    def put(ref, g, j, value):
        ref[g * GROUP : (g + 1) * GROUP, lanes(j)] = value

    def row(ref, j):
        return jnp.broadcast_to(ref[pl.ds(j, 1), :], (GROUP, LANES))

    def window(j):
        begin, stop = row(window_v.at[0], j), row(window_v.at[1], j)
        return begin, stop, [(t >= begin) & (t <= stop) for t in period]

    arrived("start", "end")
    window_v[0] = start_v[...].astype(F32)
    window_v[1] = end_v[...].astype(F32)

    arrived("dual_demand")

    @pl.loop(0, chunks)
    def _(j):
        begin, stop, active = window(j)
        parts = [jnp.where(active[g], piece(dual_demand_v, g, j), 0.0) for g in range(groups)]
        tails, total = suffix_rows(parts, sub)
        for g in range(groups):
            put(local_v, g, j, tails[g])
        own_v[0, pl.ds(j, 1), :] = total[0:1, :]

    pl.semaphore_wait(barrier, greeted)

    def remote(src, dst, send, recv, where):
        return pltpu.make_async_remote_copy(
            src_ref=src, dst_ref=dst, send_sem=send, recv_sem=recv, device_id=where, device_id_type=MESH
        )

    def part(h):
        return pl.ds(pl.multiple_of(h * half, half), half)

    sibling = place(x, z, 1 - core)
    mine, other = part(core), part(1 - core)

    def halfway(s, h):
        return remote(
            own_v.at[s, part(h)], sibling_v.at[s, part(h)], core_send.at[s, h], core_recv.at[s, h], sibling
        )

    def along(s, src, e):
        return remote(
            src, along_z_v.at[s, z], z_send.at[s, e], z_recv.at[s, z], place(x, lax.rem(z + e, nz), core)
        )

    def from_along(s, e):
        there = lax.rem(z + e, nz)
        remote(
            along_z_v.at[s, there],
            along_z_v.at[s, there],
            z_send.at[s, e],
            z_recv.at[s, there],
            place(x, there, core),
        ).wait_recv()
        return along_z_v[s, there]

    def raw(d, c):
        return remote(
            own_v.at[0, part(c)],
            raw_x_v.at[x, core],
            raw_send.at[d, c],
            raw_recv.at[x, core],
            place(lax.rem(x + d, nx), z, c),
        )

    def across(d, c):
        return remote(
            along_x_v.at[x, other],
            along_x_v.at[x, other],
            x_send.at[d, c],
            x_recv.at[x, 1 - core],
            place(lax.rem(x + d, nx), z, c),
        )

    def inside(s, where):
        return remote(
            inside_v.at[s, where], inside_v.at[s, where], inside_send.at[s], inside_recv.at[s], sibling
        )

    def column(e):
        there = lax.rem(z + e, nz)
        return along(0, column_v.at[jnp.where(z > there, 1, 0)], e)

    later_core = core == 0

    def suffix_scan(during_x, during_z):
        for d in far_first(nx):

            @pl.when(x > lax.rem(x + d, nx))
            def _():
                for c in range(CORES):
                    raw(d, c).start()

        halfway(0, 1 - core).start()
        halfway(0, core).start()
        for e in (RELAY, nz - RELAY):
            pl.semaphore_signal(
                ready, inc=1, device_id=place(x, lax.rem(z + e, nz), core), device_id_type=MESH
            )
        during_x()
        halfway(0, core).wait_recv()
        column_v[0] = jnp.zeros((half, LANES), F32)
        for d in reversed(far_first(nx)):
            there = lax.rem(x + d, nx)

            @pl.when(there > x)
            def _():
                for c in range(CORES):
                    remote(
                        raw_x_v.at[there, c],
                        raw_x_v.at[there, c],
                        raw_send.at[d, c],
                        raw_recv.at[there, c],
                        place(there, z, c),
                    ).wait_recv()
                column_v[0] += raw_x_v[there, 0] + raw_x_v[there, 1]

        column_v[1] = column_v[0] + (own_v[0, mine, :] + sibling_v[0, mine, :])
        pl.semaphore_wait(ready, 2)
        for e in far_first(nz):
            column(e).start()
        during_z()
        total = column_v[0]
        for e in reversed(far_first(nz)):
            total = total + from_along(0, e)
        inside_v[0, mine, :] = total
        inside(0, mine).start()
        window_v[2, mine, :] = total + jnp.where(later_core, sibling_v[0, mine, :], 0.0)

    def suffix_other():
        halfway(0, 1 - core).wait_recv()
        inside(0, other).wait_recv()
        window_v[2, other, :] = inside_v[0, other, :] + jnp.where(
            later_core, sibling_v[0, other, :], 0.0
        )

    def suffix_left():
        for d in far_first(nx):

            @pl.when(x > lax.rem(x + d, nx))
            def _():
                for c in range(CORES):
                    raw(d, c).wait_send()

        for h in range(CORES):
            halfway(0, h).wait_send()
        for e in far_first(nz):
            column(e).wait_send()
        inside(0, mine).wait_send()

    def prefix_scan(during_z, during_x):
        halfway(1, 1 - core).wait_recv()
        along_z_v[1, z] = own_v[1, other, :] + sibling_v[1, other, :]
        for e in far_first(nz):
            along(1, along_z_v.at[1, z], e).start()
        during_z()
        whole = along_z_v[1, z]
        partial = jnp.zeros_like(whole)
        for e in reversed(far_first(nz)):
            term = from_along(1, e)
            whole = whole + term
            partial = partial + jnp.where(lax.rem(z + e, nz) < z, term, 0.0)
        inside_v[1, other, :] = partial
        inside(1, other).start()
        along_x_v[x, other, :] = whole
        for d in far_first(nx):

            @pl.when(x < lax.rem(x + d, nx))
            def _():
                for c in range(CORES):
                    across(d, c).start()

        during_x()
        halfway(1, core).wait_recv()
        inside(1, mine).wait_recv()
        for h in range(CORES):
            halfway(1, h).wait_send()
        for e in far_first(nz):
            along(1, along_z_v.at[1, z], e).wait_send()
        window_v[3] = inside_v[1] + jnp.where(later_core, 0.0, sibling_v[1])
        for d in reversed(far_first(nx)):
            there = lax.rem(x + d, nx)

            @pl.when(there < x)
            def _():
                for h in range(CORES):
                    remote(
                        along_x_v.at[there, part(h)],
                        along_x_v.at[there, part(h)],
                        x_send.at[d, h],
                        x_recv.at[there, h],
                        place(there, z, h),
                    ).wait_recv()
                window_v[3] += along_x_v[there]

        inside(1, other).wait_send()
        for d in far_first(nx):

            @pl.when(x < lax.rem(x + d, nx))
            def _():
                for c in range(CORES):
                    across(d, c).wait_send()

    wide = 4

    def pull():
        arrived("block", "dual_resource", "coef_production", "coef_setup")
        by_block_production = exact(dual_resource_v[...], coef_production_v[...], ((1,), (1,)))
        by_block_setup = exact(dual_resource_v[...], coef_setup_v[...], ((1,), (1,)))
        stacked = jnp.concatenate(
            [t.astype(F32) for t in halves(by_block_production, 3) + halves(by_block_setup, 3)], axis=0
        ).astype(BF16)

        @pl.loop(0, chunks // wide)
        def _(i):
            for k in range(wide):
                j = i * wide + k
                ids = jnp.broadcast_to(block_v[pl.ds(j, 1), :], (blocks, LANES))
                hot = ids == lax.broadcasted_iota(jnp.int32, (blocks, LANES), 0)
                onehot_v[:, lanes(j)] = jnp.where(hot, 1.0, 0.0).astype(BF16)
            at = pl.ds(pl.multiple_of(i * wide * LANES, wide * LANES), wide * LANES)
            pulled = jnp.dot(stacked, onehot_v[:, at], preferred_element_type=F32)
            pull_production_v[:, at] = pulled[0:rows] + (
                pulled[rows : 2 * rows] + pulled[2 * rows : 3 * rows]
            )
            pull_setup_v[:, at] = pulled[3 * rows : 4 * rows] + (
                pulled[4 * rows : 5 * rows] + pulled[5 * rows : 6 * rows]
            )

    def used(bar_v, coef_v):
        deep = DEPTH * LANES

        def add_blocks(i, total):
            at = pl.ds(pl.multiple_of(i * deep, deep), deep)
            left = jnp.concatenate(halves(bar_v[:, at], 2), axis=0)
            return total + lax.dot_general(
                left, onehot_v[:, at], (((1,), (1,)), ((), ())), preferred_element_type=F32
            )

        by_block = lax.fori_loop(0, items // deep, add_blocks, jnp.zeros((2 * rows, blocks), F32))
        return exact(by_block[0:rows] + by_block[rows : 2 * rows], coef_v[...], ((1,), (0,)))

    def own_part():
        arrived(
            "cost_setup",
            "penalty",
            "dual_link",
            "setup",
            "fixing",
            "shortage",
            "production",
            "cost_production",
            "demand",
        )

        @pl.loop(0, chunks)
        def _(j):
            begin, stop, active = window(j)
            setup_price = row(cost_setup_v, j)
            late_price = row(penalty_v, j)
            fixed = jnp.zeros((GROUP, LANES), F32)
            for g in range(groups):
                on = active[g]
                dual_active = jnp.where(on, piece(dual_demand_v, g, j), 0.0)
                link_active = jnp.where(on, piece(dual_link_v, g, j), 0.0)
                primal_step = 1.0 / (2.0 + jnp.maximum(stop - period[g], 0.0))
                dual_step = 1.0 / (2.0 + jnp.maximum(period[g] - begin, 0.0))
                price = (
                    piece(cost_production_v, g, j)
                    - piece(local_v, g, j)
                    + link_active
                    + piece(pull_production_v, g, j)
                )
                before = piece(given_v, g, j)
                put(local_v, g, j, jnp.where(on, before - primal_step * price, 0.0))
                put(primal_step_v, g, j, jnp.where(on, primal_step, 0.0))
                fixed = fixed + jnp.where(on, before + piece(demand_v, g, j), 0.0)
                put(dual_step_v, g, j, dual_step)
                before = piece(setup_v, g, j)
                moved = jnp.clip(
                    before - setup_step * (setup_price - big_m * link_active + piece(pull_setup_v, g, j)),
                    0.0,
                    1.0,
                )
                state = piece(fixing_v, g, j)
                moved = jnp.where(state == 1, 0.0, jnp.where(state == 2, 1.0, moved))
                moved = jnp.where(on, moved, 0.0)
                put(setup_v, g, j, moved)
                setup_bar = jnp.where(on, 2.0 * moved - before, 0.0)
                put(setup_bar_v, g, j, setup_bar)
                put(link_v, g, j, link_active - link_step * big_m * setup_bar)
                before = piece(shortage_v, g, j)
                late = jnp.where(
                    on, jnp.maximum(before - short_step * (late_price - dual_active), 0.0), 0.0
                )
                put(shortage_v, g, j, late)
                put(dual_demand_v, g, j, dual_active - dual_step * (2.0 * late - before))
            fixed_v[pl.ds(j, 1), :] = jnp.sum(fixed, axis=0, keepdims=True)

    def own_and_usage():
        own_part()
        usage_v[y] = used(setup_bar_v, coef_setup_v)

    suffix_scan(pull, own_and_usage)
    def net_production(j):
        carry = row(window_v.at[2], j)
        total = jnp.zeros((GROUP, LANES), F32)
        for g in range(groups):
            made = jnp.maximum(piece(local_v, g, j) + piece(primal_step_v, g, j) * carry, 0.0)
            put(production_v, g, j, made)
            total = total + made
        own_v[1, pl.ds(j, 1), :] = (
            2.0 * jnp.sum(total, axis=0, keepdims=True) - fixed_v[pl.ds(j, 1), :]
        )

    def net_half(h):
        @pl.loop(0, half // UNROLL)
        def _(i):
            for k in range(UNROLL):
                net_production(h * half + i * UNROLL + k)

        halfway(1, h).start()

    net_half(core)
    suffix_other()
    net_half(1 - core)

    def beside(d):
        return remote(
            usage_v.at[y], usage_v.at[y], y_send.at[d], y_recv.at[y], place(x, z, core, lax.rem(y + d, ny))
        )

    def dual_part():
        @pl.loop(0, chunks // wide)
        def _(i):
            for k in range(wide):
                j = i * wide + k
                begin, stop, active = window(j)
                for g in range(groups):
                    bar = 2.0 * piece(production_v, g, j) - piece(given_v, g, j)
                    put(prod_bar_v, g, j, jnp.where(active[g], bar, 0.0))

        usage_v[y] += used(prod_bar_v, coef_production_v)
        for d in range(1, ny):
            beside(d).start()

        @pl.loop(0, chunks)
        def _(j):
            begin, stop, active = window(j)
            flow = [
                piece(prod_bar_v, g, j) - jnp.where(active[g], piece(demand_v, g, j), 0.0)
                for g in range(groups)
            ]
            heads = prefix_rows(flow, sub)
            for g in range(groups):
                put(
                    dual_demand_v,
                    g,
                    j,
                    piece(dual_demand_v, g, j) - piece(dual_step_v, g, j) * heads[g],
                )
                link = jnp.maximum(piece(link_v, g, j) + link_step * piece(prod_bar_v, g, j), 0.0)
                put(dual_link_v, g, j, jnp.where(active[g], link, 0.0))

    def resource_part():
        for d in range(1, ny):
            beside(d).wait_send()
        for d in range(1, ny):
            there = lax.rem(y + d, ny)
            remote(
                usage_v.at[there], usage_v.at[there], y_send.at[d], y_recv.at[there], place(x, z, core, there)
            ).wait_recv()
        arrived("capacity")
        usage = usage_v[0]
        for k in range(1, ny):
            usage = usage + usage_v[k]
        scale = dual_resource_v.shape[1] / items_total
        dual_resource_v[...] = jnp.maximum(dual_resource_v[...] + scale * (usage - capacity_v[...]), 0.0)

    def dual_and_left():
        dual_part()
        suffix_left()

    prefix_scan(dual_and_left, resource_part)


def finish(
    production_v,
    setup_v,
    shortage_v,
    dual_demand_v,
    dual_link_v,
    dual_resource_v,
    dual_step_v,
    window_v,
    production_o,
    setup_o,
    shortage_o,
    dual_demand_o,
    dual_link_o,
    dual_resource_o,
    result_v,
    out_sem,
):
    pairs = [
        (production_v, production_o),
        (setup_v, setup_o),
        (shortage_v, shortage_o),
        (dual_link_v, dual_link_o),
        (dual_resource_v, dual_resource_o),
    ]
    copies = [pltpu.make_async_copy(src, dst, out_sem.at[k]) for k, (src, dst) in enumerate(pairs)]
    for copy in copies:
        copy.start()
    rows, items = result_v.shape
    first = (lax.axis_index("tm") * rows).astype(F32)
    sub = lax.broadcasted_iota(jnp.int32, (GROUP, LANES), 0).astype(F32)

    step = items // PIECES
    for p in range(PIECES):

        @pl.loop(p * step // LANES, (p + 1) * step // LANES, step=2)
        def _(i):
            for j in (i, i + 1):
                at = pl.ds(pl.multiple_of(j * LANES, LANES), LANES)
                begin, stop, carry = [
                    jnp.broadcast_to(window_v[k, pl.ds(j, 1), :], (GROUP, LANES)) for k in (0, 1, 3)
                ]
                for g in range(rows // GROUP):
                    t = sub + (first + float(g * GROUP))
                    band = slice(g * GROUP, (g + 1) * GROUP)
                    dual = jnp.maximum(dual_demand_v[band, at] - dual_step_v[band, at] * carry, 0.0)
                    result_v[band, at] = jnp.where((t >= begin) & (t <= stop), dual, 0.0)

        at = pl.ds(p * step, step)
        copies.append(
            pltpu.make_async_copy(result_v.at[:, at], dual_demand_o.at[:, at], out_sem.at[len(pairs) + p])
        )
        copies[-1].start()

    for copy in copies:
        copy.wait()


def shards(ranks, items_total, *args):
    (
        production,
        setup,
        shortage,
        dual_demand,
        dual_link,
        dual_resource,
        cost_production,
        cost_setup,
        penalty,
        demand,
        capacity,
        coef_production,
        coef_setup,
        horizon_start,
        horizon_end,
        fixing,
        block_id,
    ) = args
    nx, nz, ny = ranks
    rows, items = production.shape
    resources = dual_resource.shape[1]
    blocks = coef_production.shape[0]
    chunks = items // LANES
    per_item = (chunks, LANES)
    big, vector, small = (rows, items), (chunks, LANES), (rows, resources)

    def vmem(shape, dtype=F32):
        return pltpu.VMEM(shape, dtype)

    dma = pltpu.SemaphoreType.DMA
    anywhere = pl.BlockSpec(memory_space=pl.ANY)
    scratch = (
        [vmem(big)] * 2
        + [vmem(big, jnp.int32)]
        + [vmem(small)]
        + [vmem((blocks, resources))] * 2
        + [vmem(vector)] * 2
        + [vmem(vector, jnp.int32)] * 3
        + [vmem((blocks, items), BF16)]
        + [vmem(big)] * 5
        + [vmem(vector)]
        + [vmem(big)] * 3
        + [
            vmem((2,) + vector),
            vmem((2,) + vector),
            vmem((2, nz, chunks // 2, LANES)),
            vmem((nx,) + vector),
            vmem((2,) + vector),
            vmem((nx, CORES, chunks // 2, LANES)),
            vmem((2, chunks // 2, LANES)),
            vmem((ny,) + small),
        ]
        + [
            dma((17,)),
            dma((2, CORES)),
            dma((2, CORES)),
            dma((2, nz)),
            dma((2, nz)),
            dma((nx, CORES)),
            dma((nx, CORES)),
            dma((2,)),
            dma((2,)),
            dma((nx, CORES)),
            dma((nx, CORES)),
            pltpu.SemaphoreType.REGULAR,
            dma((ny,)),
            dma((ny,)),
        ]
    )
    operands = [
        production,
        setup,
        shortage,
        dual_demand,
        dual_link,
        dual_resource,
        cost_production,
        cost_setup.reshape(per_item),
        penalty.reshape(per_item),
        demand,
        capacity,
        coef_production,
        coef_setup,
        horizon_start.reshape(per_item),
        horizon_end.reshape(per_item),
        fixing,
        block_id.reshape(per_item),
    ]
    operands = [pltpu.with_memory_space_constraint(a, pltpu.HBM) for a in operands]
    held = pl.BlockSpec(memory_space=pltpu.VMEM)
    between = [big] * 5 + [small, big, (4,) + vector]
    parts = pl.pallas_call(
        functools.partial(kernel, ranks, items_total),
        out_shape=[pltpu.VMEM(shape, F32) for shape in between],
        in_specs=[anywhere] * 17,
        out_specs=[held] * len(between),
        scratch_shapes=scratch,
        compiler_params=pltpu.CompilerParams(
            collective_id=0, has_side_effects=True, vmem_limit_bytes=40 * 1024 * 1024
        ),
        name="lot_step",
    )(*operands)
    results = pl.pallas_call(
        finish,
        out_shape=[jax.ShapeDtypeStruct(big, F32)] * 5 + [jax.ShapeDtypeStruct(small, F32)],
        in_specs=[held] * len(between),
        out_specs=[anywhere] * 6,
        scratch_shapes=[vmem(big), dma((5 + PIECES,))],
        compiler_params=pltpu.CompilerParams(vmem_limit_bytes=8 * 1024 * 1024),
        name="finish",
    )(*parts)
    return tuple(results)


def solution(mesh):
    across, ny = mesh.shape["tm"], mesh.shape["items"]
    nz = 8
    nx = across // (nz * CORES)
    placed = (
        P("tm", "items"),
        P("tm", "items"),
        P("tm", "items"),
        P("tm", "items"),
        P("tm", "items"),
        P("tm", None),
        P("tm", "items"),
        P("items"),
        P("items"),
        P("tm", "items"),
        P("tm", None),
        P(),
        P(),
        P("items"),
        P("items"),
        P("tm", "items"),
        P("items"),
    )

    def step(*args):
        return jax.shard_map(
            functools.partial(shards, (nx, nz, ny), args[0].shape[1]),
            mesh=mesh,
            in_specs=placed,
            out_specs=(P("tm", "items"),) * 5 + (P("tm", None),),
            check_vma=False,
        )(*args)

    return step
```
